128 devices in a mesh: dp: 4 (over y), fsdp: 32 (over z, x, core).
Axes of the slice: x: 4, y: 4, z: 4, core: 2. Of those that a mesh axis runs over, the one named last changes fastest.
Arguments:
- block_input: bfloat16 [2, 16384, 1024], P(None, ('dp', 'fsdp')), may hold values from -6 to 6
- cotangent: bfloat16 [2, 16384, 1024], P(None, ('dp', 'fsdp')), may hold values from -6 to 6
- in_weight: float32 [1024, 3072], P('fsdp'), may hold values from -0.1875 to 0.1875
- out_weight: float32 [1024, 1024], P('fsdp'), may hold values from -0.1875 to 0.1875
- gate_weight: float32 [1024, 4608], P('fsdp'), may hold values from -0.1875 to 0.1875
- up_weight: float32 [1024, 4608], P('fsdp'), may hold values from -0.1875 to 0.1875
- down_weight: float32 [4608, 1024], P('fsdp'), may hold values from -0.09375 to 0.09375
- small_params: float32 [5, 1024], P(None, 'fsdp'), may hold values from 0.25 to 1.75
- in_first: float32 [1024, 3072], P('fsdp'), may hold values from -256 to 256
- out_first: float32 [1024, 1024], P('fsdp'), may hold values from -256 to 256
- gate_first: float32 [1024, 4608], P('fsdp'), may hold values from -32 to 32
- up_first: float32 [1024, 4608], P('fsdp'), may hold values from -32 to 32
- down_first: float32 [4608, 1024], P('fsdp'), may hold values from -80 to 80
- small_first: float32 [5, 1024], P(None, 'fsdp'), may hold values from -256 to 256
- in_second: float32 [1024, 3072], P('fsdp'), may hold values from 10485.76 to 41287.68
- out_second: float32 [1024, 1024], P('fsdp'), may hold values from 10485.76 to 41287.68
- gate_second: float32 [1024, 4608], P('fsdp'), may hold values from 137.6256 to 557.056
- up_second: float32 [1024, 4608], P('fsdp'), may hold values from 137.6256 to 557.056
- down_second: float32 [4608, 1024], P('fsdp'), may hold values from 720.896 to 2883.584
- small_second: float32 [5, 1024], P(None, 'fsdp'), may hold values from 6881.28 to 27525.12
Outputs:
- block_output: bfloat16 [2, 16384, 1024], P(None, ('dp', 'fsdp'))
- input_grad: float32 [2, 16384, 1024], P(None, ('dp', 'fsdp'))
- new_in_weight: float32 [1024, 3072], P('fsdp')
- new_out_weight: float32 [1024, 1024], P('fsdp')
- new_gate_weight: float32 [1024, 4608], P('fsdp')
- new_up_weight: float32 [1024, 4608], P('fsdp')
- new_down_weight: float32 [4608, 1024], P('fsdp')
- new_small_params: float32 [5, 1024], P(None, 'fsdp')
- new_in_first: float32 [1024, 3072], P('fsdp')
- new_out_first: float32 [1024, 1024], P('fsdp')
- new_gate_first: float32 [1024, 4608], P('fsdp')
- new_up_first: float32 [1024, 4608], P('fsdp')
- new_down_first: float32 [4608, 1024], P('fsdp')
- new_small_first: float32 [5, 1024], P(None, 'fsdp')
- new_in_second: float32 [1024, 3072], P('fsdp')
- new_out_second: float32 [1024, 1024], P('fsdp')
- new_gate_second: float32 [1024, 4608], P('fsdp')
- new_up_second: float32 [1024, 4608], P('fsdp')
- new_down_second: float32 [4608, 1024], P('fsdp')
- new_small_second: float32 [5, 1024], P(None, 'fsdp')
The draws below stay inside these ranges and needn't reach their ends.
All inputs are finite; a program needn't handle non-finite values.
Results may differ from the reference program's by a relative error of at most 0.023.
Values may be sent and summed in bfloat16 or wider, within the bound.
A program may use at most 192 MiB of HBM per device.

```python
import math
import jax
import jax.numpy as jnp
from jax import lax

D = 1024
FF = 4608
KW = 3
MICRO = 2
STEP = 10
SEQ = 4096
TOKENS = 16384


def shard_levels(key, dims, shards, low, top_value):
    def one(axis_at, shards_of):
        draws = jax.random.uniform(jax.random.fold_in(jax.random.fold_in(key, 6), axis_at), (shards_of,), jnp.float32, low / len(shards), top_value / len(shards))
        return jnp.repeat(jnp.exp(draws), dims[axis_at] // shards_of).reshape((-1,) + (1,) * (len(dims) - axis_at - 1))

    level = one(*shards[0])
    for cut in shards[1:]:
        level = level * one(*cut)
    return level


def normal_values(stream_key, shape, scale, bound, split=(), dtype=jnp.bfloat16):
    array = jax.random.normal(stream_key, shape, jnp.float32) * scale
    if len(split) > 0:
        array = shard_levels(stream_key, shape, split, -0.22, 0.18) * array
    return jnp.clip(array, min=-bound, max=bound).astype(dtype)


def setup_inputs(seed: int = 0) -> dict:
    arg_keys = jax.random.split(jax.random.key(seed), 21)
    return {
        "block_input": normal_values(arg_keys[0], (MICRO, TOKENS, D), 1.0, 6.0, ((1, 128),)),
        "cotangent": normal_values(arg_keys[1], (MICRO, TOKENS, D), 1.0, 6.0, ((1, 128),)),
        "in_weight": normal_values(arg_keys[2], (D, 3 * D), D ** -0.5, 0.1875, ((0, 32),), jnp.float32),
        "out_weight": normal_values(arg_keys[3], (D, D), D ** -0.5, 0.1875, ((0, 32),), jnp.float32),
        "gate_weight": normal_values(arg_keys[4], (D, FF), D ** -0.5, 0.1875, ((0, 32),), jnp.float32),
        "up_weight": normal_values(arg_keys[5], (D, FF), D ** -0.5, 0.1875, ((0, 32),), jnp.float32),
        "down_weight": normal_values(arg_keys[6], (FF, D), FF ** -0.5, 0.09375, ((0, 32),), jnp.float32),
        "small_params": jnp.clip(1.0 + 0.15 * jax.random.normal(arg_keys[7], (KW + 2, D), jnp.float32), 0.25, 1.75),
        "in_first": normal_values(arg_keys[8], (D, 3 * D), (0.27 * (MICRO * TOKENS) ** 0.5), 256.0, ((0, 32),), jnp.float32),
        "out_first": normal_values(arg_keys[9], (D, D), (0.27 * (MICRO * TOKENS) ** 0.5), 256.0, ((0, 32),), jnp.float32),
        "gate_first": normal_values(arg_keys[10], (D, FF), (0.031 * (MICRO * TOKENS) ** 0.5), 32.0, ((0, 32),), jnp.float32),
        "up_first": normal_values(arg_keys[11], (D, FF), (0.031 * (MICRO * TOKENS) ** 0.5), 32.0, ((0, 32),), jnp.float32),
        "down_first": normal_values(arg_keys[12], (FF, D), (0.072 * (MICRO * TOKENS) ** 0.5), 80.0, ((0, 32),), jnp.float32),
        "small_first": normal_values(arg_keys[13], (KW + 2, D), (0.22 * (MICRO * TOKENS) ** 0.5), 256.0, ((1, 32),), jnp.float32),
        "in_second": jnp.clip(jnp.exp(math.log(41287.68) - 1.370546 * jax.random.uniform(arg_keys[14], (D, 3 * D), jnp.float32) ** shard_levels(arg_keys[14], (D, 3 * D), ((0, 32),), -0.2, 0.2)), 10485.76, 41287.68),
        "out_second": jnp.clip(jnp.exp(math.log(41287.68) - 1.370546 * jax.random.uniform(arg_keys[15], (D, D), jnp.float32) ** shard_levels(arg_keys[15], (D, D), ((0, 32),), -0.2, 0.2)), 10485.76, 41287.68),
        "gate_second": jnp.clip(jnp.exp(math.log(557.056) - 1.3981289 * jax.random.uniform(arg_keys[16], (D, FF), jnp.float32) ** shard_levels(arg_keys[16], (D, FF), ((0, 32),), -0.2, 0.2)), 137.6256, 557.056),
        "up_second": jnp.clip(jnp.exp(math.log(557.056) - 1.3981289 * jax.random.uniform(arg_keys[17], (D, FF), jnp.float32) ** shard_levels(arg_keys[17], (D, FF), ((0, 32),), -0.2, 0.2)), 137.6256, 557.056),
        "down_second": jnp.clip(jnp.exp(math.log(2883.584) - 1.3862944 * jax.random.uniform(arg_keys[18], (FF, D), jnp.float32) ** shard_levels(arg_keys[18], (FF, D), ((0, 32),), -0.2, 0.2)), 720.896, 2883.584),
        "small_second": jnp.clip(jnp.exp(math.log(27525.12) - 1.3862944 * jax.random.uniform(arg_keys[19], (KW + 2, D), jnp.float32) ** shard_levels(arg_keys[19], (KW + 2, D), ((1, 32),), -0.2, 0.2)), 6881.28, 27525.12),
    }


norm_eps = 1e-05
beta_one = 0.9
beta_two = 0.95
adam_eps = 1e-08
rate_matrix = 0.02
rate_small = 0.4
weight_decay = 0.1

@jax.custom_vjp
def low(v):
    return lax.optimization_barrier(v.astype(jnp.bfloat16)).astype(jnp.float32)

@jax.custom_vjp
def low_back(v):
    return v

def low_keep(v):
    return (low(v), None)

def low_pass(kept, grad):
    return (grad,)

def back_keep(v):
    return (v, None)

def back_low(kept, grad):
    return (low(grad),)
low.defvjp(low_keep, low_pass)
low_back.defvjp(back_keep, back_low)

def product(left, right):
    return jnp.dot(left, right, precision=lax.Precision.HIGHEST, preferred_element_type=jnp.float32)

def forward_sequence(tokens_in, in_weight, out_weight, gate_weight, up_weight, down_weight, small_params):
    in_low = low(in_weight)
    out_low = low(out_weight)
    gate_low = low(gate_weight)
    up_low = low(up_weight)
    down_low = low(down_weight)
    small_low = low(small_params)
    conv_taps = small_low[0:KW]
    gain_first = small_low[KW]
    gain_second = small_low[KW + 1]
    scale_first = lax.rsqrt(lax.optimization_barrier(jnp.mean(tokens_in * tokens_in, axis=-1, keepdims=True)) + norm_eps)
    normed_first = low(tokens_in * scale_first * gain_first)
    projected = low_back(product(normed_first, in_low))
    gate_b = projected[:, 0:D]
    gate_c = projected[:, D:2 * D]
    values = projected[:, 2 * D:3 * D]
    mixed_in = low(gate_b * values)
    padded = jnp.pad(mixed_in, ((KW - 1, 0), (0, 0)))
    conv_out = jnp.zeros((SEQ, D), jnp.float32)
    for offset in range(KW):
        conv_out = conv_out + conv_taps[offset] * padded[KW - 1 - offset:KW - 1 - offset + SEQ]
    conv_out = low_back(conv_out)
    gated_out = low(gate_c * conv_out)
    branch = low_back(product(gated_out, out_low))
    middle = tokens_in + branch
    scale_second = lax.rsqrt(lax.optimization_barrier(jnp.mean(middle * middle, axis=-1, keepdims=True)) + norm_eps)
    normed_second = low(middle * scale_second * gain_second)
    gate_pre = low_back(product(normed_second, gate_low))
    up_pre = low_back(product(normed_second, up_low))
    hidden_act = low(jax.nn.silu(gate_pre) * up_pre)
    return middle + product(hidden_act, down_low)

def adam_update(weight, first, second, gradient, step_rate, decay_rate):
    first_new = beta_one * first + (1.0 - beta_one) * gradient
    second_new = beta_two * second + (1.0 - beta_two) * gradient * gradient
    corrected = first_new / (1.0 - beta_one ** STEP) / (jnp.sqrt(second_new / (1.0 - beta_two ** STEP)) + adam_eps)
    return (weight - step_rate * (corrected + decay_rate * weight), first_new, second_new)

def reference(block_input, cotangent, in_weight, out_weight, gate_weight, up_weight, down_weight, small_params, in_first, out_first, gate_first, up_first, down_first, small_first, in_second, out_second, gate_second, up_second, down_second, small_second):
    seq_count = MICRO * TOKENS // SEQ
    tokens_all = block_input.astype(jnp.float32).reshape(seq_count, SEQ, D)
    cotangents = cotangent.astype(jnp.float32).reshape(seq_count, SEQ, D)
    weights = (in_weight, out_weight, gate_weight, up_weight, down_weight, small_params)

    def visit(totals, scan_item):
        tokens_in, grad_out = scan_item
        result, pullback = jax.vjp(forward_sequence, tokens_in, *weights)
        pulled = pullback(grad_out)
        totals = tuple((running + grad_piece for running, grad_piece in zip(totals, pulled[1:])))
        return (totals, (result.astype(jnp.bfloat16), pulled[0]))
    initial = tuple((jnp.zeros_like(weight) for weight in weights))
    totals, (outputs, grads_in) = lax.scan(visit, initial, (tokens_all, cotangents))
    new_in = adam_update(in_weight, in_first, in_second, totals[0], rate_matrix, weight_decay)
    new_out = adam_update(out_weight, out_first, out_second, totals[1], rate_matrix, weight_decay)
    new_gate = adam_update(gate_weight, gate_first, gate_second, totals[2], rate_matrix, weight_decay)
    new_up = adam_update(up_weight, up_first, up_second, totals[3], rate_matrix, weight_decay)
    new_down = adam_update(down_weight, down_first, down_second, totals[4], rate_matrix, weight_decay)
    new_small = adam_update(small_params, small_first, small_second, totals[5], rate_small, 0.0)
    return (outputs.reshape(MICRO, TOKENS, D), grads_in.reshape(MICRO, TOKENS, D), new_in[0], new_out[0], new_gate[0], new_up[0], new_down[0], new_small[0], new_in[1], new_out[1], new_gate[1], new_up[1], new_down[1], new_small[1], new_in[2], new_out[2], new_gate[2], new_up[2], new_down[2], new_small[2])
```

```python
import functools

import jax
import jax.numpy as jnp
from jax import lax
from jax.experimental import pallas as pl
from jax.experimental.pallas import tpu as pltpu
from jax.sharding import PartitionSpec as P

MESH = pl.DeviceIdType.MESH
KW = 3
MICRO = 2
STEP = 10

norm_eps = 1e-05
beta_one = 0.9
beta_two = 0.95
adam_eps = 1e-08
rate_matrix = 0.02
rate_small = 0.4
weight_decay = 0.1

MATS = ("in", "out", "gate", "up", "down")
THIRDS = {"in": 3, "out": 2, "gate": 3, "up": 3, "down": 3}
FULL = {
    "in": (3, 4, 4, 4, 2, 32, 256),
    "out": (4, 4, 4, 2, 2, 16, 256),
    "gate": (3, 4, 4, 4, 2, 32, 384),
    "up": (3, 4, 4, 4, 2, 32, 384),
    "down": (4, 4, 4, 2, 3, 48, 256),
}
OWN = {
    "in": (3, 4, 32, 256),
    "out": (4, 2, 16, 256),
    "gate": (3, 4, 32, 384),
    "up": (3, 4, 32, 384),
    "down": (4, 3, 48, 256),
}
BLOCK = {"in": (32, 256), "out": (16, 256), "gate": (32, 384), "up": (32, 384), "down": (48, 256)}
BY_THIRD = ("in", "gate", "up")
GATHER_ORDER = {0: ("z", "x"), 1: ("x", "y", "z"), 2: ("z", "x", "y")}
SUM_ORDER = {0: ("x", "z", "y"), 1: ("z", "y", "x"), 2: ("y", "x", "z")}
ALL = slice(None)
VMEM_BYTES = 62 * 1024 * 1024


def coords():
    y = lax.axis_index("dp")
    f = lax.axis_index("fsdp")
    return {"y": y, "z": f // 8, "x": (f // 2) % 4, "c": f % 2}


def device(at):
    return (at["y"], at["z"] * 8 + at["x"] * 2 + at["c"])


def shifted(at, axis, by):
    new = dict(at)
    new[axis] = (at[axis] + by) % (2 if axis == "c" else 4)
    return new


def meet(me):
    sem = pltpu.get_barrier_semaphore()
    peers = [shifted(me, "c", 1)] + [shifted(me, a, s) for a in "xyz" for s in (1, 2, 3)]
    for p in peers:
        pl.semaphore_signal(sem, inc=1, device_id=device(p), device_id_type=MESH)
    pl.semaphore_wait(sem, len(peers))


def half_of(name, half):
    if name in BY_THIRD:
        return (ALL if half is None else pl.ds(16 * half, 16), ALL)
    return (ALL, ALL if half is None else pl.ds(128 * half, 128))


def view(ref, name, t, at, half=None):
    tail = half_of(name, half)
    if name in BY_THIRD:
        return ref.at[(t, at["y"], at["z"], at["x"], at["c"]) + tail]
    return ref.at[(at["y"], at["z"], at["x"], at["c"], t) + tail]


def own_view(ref, name, t, q=ALL):
    if name in BY_THIRD:
        return ref.at[t, q]
    return ref.at[q, t]


class Links:
    def __init__(self, me, send_sem, recv_sem):
        self.me, self.send_sem, self.recv_sem = me, send_sem, recv_sem
        self.sent = []

    def send(self, src, dst, axis, by):
        i = len(self.sent)
        cp = pltpu.make_async_remote_copy(
            src,
            dst,
            self.send_sem.at[i],
            self.recv_sem.at[i],
            device_id=device(shifted(self.me, axis, by)),
            device_id_type=MESH,
        )
        cp.start()
        self.sent.append(cp)
        return cp

    def finish(self):
        for cp in self.sent:
            cp.wait_send()


def gather_kernel(*refs):
    own = dict(zip(MATS, refs[:5]))
    small_own = refs[5]
    full = dict(zip(MATS, refs[6:11]))
    small_full, local_sem, send_sem, recv_sem = refs[11:]
    me = coords()
    links = Links(me, send_sem, recv_sem)
    units = [(name, t) for name in MATS for t in range(THIRDS[name])]

    copies = []
    for k, (name, t) in enumerate(units):
        q = ALL if t == 0 else me["y"]
        src, dst = own_view(own[name], name, t, q), view(full[name], name, t, dict(me, y=q))
        copies.append(pltpu.make_async_copy(src, dst, local_sem.at[k]))
    mine = small_full.at[me["z"], me["x"], me["c"]]
    copies.append(pltpu.make_async_copy(small_own, mine, local_sem.at[len(units)]))
    for cp in copies:
        cp.start()
    meet(me)
    for cp in copies:
        cp.wait()

    def send(u, at, axis, by, half=None):
        piece = view(full[u[0]], u[0], u[1], at, half)
        return links.send(piece, piece, axis, by)

    def send_small(at, axis, steps):
        piece = small_full.at[at["z"], at["x"], at["c"]]
        return [links.send(piece, piece, axis, s) for s in steps]

    at_of = {u: dict(me, y=ALL) if u[1] == 0 else dict(me) for u in units}
    small_at = dict(me)
    tail = []
    for phase, small_axis in enumerate("zxc"):
        active = []
        for u in units:
            order = GATHER_ORDER[u[1]]
            p = phase - (3 - len(order))
            if p >= 0:
                active.append((u, order[p], p == len(order) - 1))
        small = send_small(small_at, small_axis, (1,) if small_axis == "c" else (1, 2, 3))
        first = {}
        for u, axis, last in active:
            at = at_of[u]
            first[u] = (send(u, at, axis, 1), send(u, at, axis, 3))
            if last:
                tail.append(send(u, at, "c", 1))
        second = {}
        for u, axis, last in active:
            from_behind, from_ahead = first[u]
            behind, ahead = shifted(at_of[u], axis, 3), shifted(at_of[u], axis, 1)
            from_behind.wait_recv()
            one = send(u, behind, axis, 1, 0)
            if last:
                tail.append(send(u, behind, "c", 1))
            from_ahead.wait_recv()
            two = send(u, ahead, axis, 3, 1)
            if last:
                tail.append(send(u, ahead, "c", 1))
            second[u] = (one, two)
        for cp in small:
            cp.wait_recv()
        small_at = dict(small_at, **{small_axis: ALL})
        for u, axis, last in active:
            for cp in second[u]:
                cp.wait_recv()
            if last:
                tail.append(send(u, shifted(at_of[u], axis, 2), "c", 1))
            at_of[u] = dict(at_of[u], **{axis: ALL})
    for cp in tail:
        cp.wait_recv()
    links.finish()


def pieces(w, name):
    w = w.astype(jnp.bfloat16)
    if name in BY_THIRD:
        return w.reshape(32, 3, 4, -1).transpose(1, 2, 0, 3)
    if name == "out":
        return w.reshape(2, 16, 4, 256).transpose(2, 0, 1, 3)
    return w.reshape(3, 48, 4, 256).transpose(2, 0, 1, 3)


def joined(g, name):
    if name in BY_THIRD:
        return g.transpose(2, 0, 1, 3).reshape(32, -1)
    return g.transpose(1, 2, 0, 3).reshape(-1, 1024)


def gather(weights, small):
    own = [pieces(w, name) for w, name in zip(weights, MATS)]
    small_low = small.astype(jnp.bfloat16).astype(jnp.float32)
    small_own = jnp.pad(small_low, ((0, 3), (0, 96)))
    in_vmem = pl.BlockSpec(memory_space=pltpu.VMEM)
    anywhere = pl.BlockSpec(memory_space=pl.ANY)
    *full, small_full = pl.pallas_call(
        gather_kernel,
        out_shape=[jax.ShapeDtypeStruct(FULL[name], jnp.bfloat16) for name in MATS]
        + [jax.ShapeDtypeStruct((4, 4, 2, 8, 128), jnp.float32)],
        in_specs=[in_vmem] * 6,
        out_specs=[anywhere] * 5 + [in_vmem],
        scratch_shapes=[
            pltpu.SemaphoreType.DMA((16,)),
            pltpu.SemaphoreType.DMA((256,)),
            pltpu.SemaphoreType.DMA((256,)),
        ],
        compiler_params=pltpu.CompilerParams(collective_id=1, has_side_effects=True),
        name="gather_weights",
    )(*own, small_own)
    small_rows = small_full.reshape(32, 8, 128)[:, 0:5, 0:32]
    return full, small_rows.transpose(1, 0, 2).reshape(5, 1024)


def add_blocks(dst, count, *srcs):
    total = 1
    for n in count:
        total *= n

    def step(i, carry):
        idx = []
        rest = i
        for n in reversed(count):
            idx.insert(0, rest % n)
            rest = rest // n
        ref = dst(tuple(idx))
        value = ref[...].astype(jnp.float32)
        for src in srcs:
            value = value + src(tuple(idx))[...].astype(jnp.float32)
        ref[...] = value.astype(jnp.bfloat16)
        return carry

    lax.fori_loop(0, total, step, 0, unroll=min(4, total))


def sum_units():
    return [(name, t) for name in ("gate", "up", "down", "in", "out") for t in range(THIRDS[name])]


def phase_counts(t):
    order = SUM_ORDER[t]
    return [[a for a in "yzx" if a in order[p + 1 :]] for p in range(3)]


def landing(name, t):
    rows, cols = BLOCK[name]
    half = (rows // 2, cols) if name in BY_THIRD else (rows, cols // 2)
    shapes = []
    for rest in phase_counts(t):
        lead = (4,) * len(rest)
        shapes.append(((2,) + lead + half, (2,) + lead + (rows, cols)))
    return shapes


def reduce_kernel(*refs):
    names = MATS
    grads = dict(zip(names, refs[:5]))
    small = refs[5]
    outs = dict(zip(names, refs[6:11]))
    small_out = refs[11]
    scratch = list(refs[12:])
    mine = {name: scratch.pop(0) for name in names}
    theirs = {name: scratch.pop(0) for name in names}
    units = sum_units()
    land = {u: [(scratch.pop(0), scratch.pop(0)) for _ in range(3)] for u in units}
    small_land = scratch.pop(0)
    local_sem, send_sem, recv_sem = scratch
    me = coords()
    links = Links(me, send_sem, recv_sem)
    batches = [[u for u in units if u[0] == name] for name in ("gate", "up", "down", "in", "out")]

    def part(ref, u, at, half=None):
        name, t = u
        tail = half_of(name, half)
        if name in BY_THIRD:
            return ref.at[(t, at["y"], at["z"], at["x"]) + tail]
        return ref.at[(at["y"], at["z"], at["x"], t) + tail]

    every = {"y": ALL, "z": ALL, "x": ALL}
    loads, swaps = {}, {}
    for k, name in enumerate(names):
        pick = (ALL,) * (4 if name in BY_THIRD else 3) + (me["c"],)
        loads[name] = pltpu.make_async_copy(grads[name].at[pick], mine[name], local_sem.at[k])
    meet(me)
    for name in ("gate", "up", "down", "in", "out"):
        loads[name].start()
        pick = (ALL,) * (4 if name in BY_THIRD else 3) + (1 - me["c"],)
        swaps[name] = links.send(grads[name].at[pick], theirs[name], "c", 1)

    small_out[...] = small[...]
    small_pending = []
    small_ids = set()

    def small_send(axis, slot):
        steps = (1,) if axis == "c" else (1, 2, 3)
        small_ids.update(range(len(links.sent), len(links.sent) + len(steps)))
        small_pending.append(
            [links.send(small_out, small_land.at[slot + s - 1], axis, s) for s in steps]
        )

    def small_take(slot):
        pending = small_pending.pop(0)
        for cp in pending:
            cp.wait()
        total = small_out[...]
        for s in range(len(pending)):
            total = total + small_land[slot + s]
        small_out[...] = total

    small_steps = [("c", 0), ("x", 1), ("z", 4), ("y", 7)]

    at_of = {u: dict(every) for u in units}
    pending = {}

    def lead_of(u, p):
        return phase_counts(u[1])[p]

    def adder(u, p, at, half, *landed):
        rest = lead_of(u, p)

        def dst(idx):
            spot = dict(at)
            spot.update(zip(rest, idx))
            return part(mine[u[0]], u, spot, half)

        def src(ref):
            return lambda idx: ref.at[idx] if idx else ref

        add_blocks(dst, (4,) * len(rest), *[src(r) for r in landed])

    def start_phase(u, p):
        axis = SUM_ORDER[u[1]][p]
        far = dict(at_of[u], **{axis: (me[axis] + 2) % 4})
        halves = land[u][p][0]
        pending[u] = [
            links.send(part(mine[u[0]], u, far, 0), halves.at[0], axis, 1),
            links.send(part(mine[u[0]], u, far, 1), halves.at[1], axis, 3),
        ]

    def middle_phase(u, p):
        axis = SUM_ORDER[u[1]][p]
        halves, blocks = land[u][p]
        ahead = dict(at_of[u], **{axis: (me[axis] + 1) % 4})
        behind = dict(at_of[u], **{axis: (me[axis] + 3) % 4})
        one, two = pending[u]
        one.wait_recv()
        adder(u, p, ahead, 0, halves.at[0])
        a = links.send(part(mine[u[0]], u, ahead), blocks.at[0], axis, 1)
        two.wait_recv()
        adder(u, p, behind, 1, halves.at[1])
        b = links.send(part(mine[u[0]], u, behind), blocks.at[1], axis, 3)
        pending[u] = [a, b]

    def end_phase(u, p):
        axis = SUM_ORDER[u[1]][p]
        blocks = land[u][p][1]
        for cp in pending[u]:
            cp.wait_recv()
        at_of[u] = dict(at_of[u], **{axis: me[axis]})
        adder(u, p, at_of[u], None, blocks.at[0], blocks.at[1])

    last = []

    def stage(s, batch):
        name = batch[0][0]
        if s == 0:
            loads[name].wait()
            swaps[name].wait_recv()
            for u in batch:
                t = u[1]

                def dst(idx, u=u):
                    return part(mine[u[0]], u, dict(zip("yzx", idx)))

                def src(idx, u=u):
                    return part(theirs[u[0]], u, dict(zip("yzx", idx)))

                add_blocks(dst, (4, 4, 4), src)
                start_phase(u, 0)
            return
        p, kind = (s - 1) // 2, (s - 1) % 2
        if p < 3:
            for u in batch:
                if kind == 0:
                    middle_phase(u, p)
                else:
                    end_phase(u, p)
                    if p < 2:
                        start_phase(u, p + 1)
                    else:
                        spot = own_view(outs[u[0]], u[0], u[1], me["y"])
                        spot[...] = part(mine[u[0]], u, at_of[u])[...]
                        for by in (1, 2, 3):
                            last.append(links.send(spot, spot, "y", by))

    stages = 7
    small_send(*small_steps[0])
    for tick in range(len(batches) + stages - 1):
        if 0 < tick <= 4:
            small_take(small_steps[tick - 1][1])
            if tick < 4:
                small_send(*small_steps[tick])
        for s in range(stages):
            if 0 <= tick - s < len(batches):
                stage(s, batches[tick - s])
    for cp in last:
        cp.wait_recv()
    for i, cp in enumerate(links.sent):
        if i not in small_ids:
            cp.wait_send()


def sums(grads, small):
    in_vmem = pl.BlockSpec(memory_space=pltpu.VMEM)
    anywhere = pl.BlockSpec(memory_space=pl.ANY)
    core = {}
    for name in MATS:
        shape = list(FULL[name])
        del shape[4 if name in BY_THIRD else 3]
        core[name] = tuple(shape)
    scratch = [pltpu.VMEM(core[name], jnp.bfloat16) for name in MATS] * 2
    for u in sum_units():
        for halves, blocks in landing(*u):
            scratch += [pltpu.VMEM(halves, jnp.bfloat16), pltpu.VMEM(blocks, jnp.bfloat16)]
    scratch += [
        pltpu.VMEM((10, 8, 1024), jnp.float32),
        pltpu.SemaphoreType.DMA((8,)),
        pltpu.SemaphoreType.DMA((256,)),
        pltpu.SemaphoreType.DMA((256,)),
    ]
    *outs, small_sum = pl.pallas_call(
        reduce_kernel,
        out_shape=[jax.ShapeDtypeStruct(OWN[name], jnp.bfloat16) for name in MATS]
        + [jax.ShapeDtypeStruct((8, 1024), jnp.float32)],
        in_specs=[anywhere] * 5 + [in_vmem],
        out_specs=[in_vmem] * 6,
        scratch_shapes=scratch,
        compiler_params=pltpu.CompilerParams(
            collective_id=2, has_side_effects=True, vmem_limit_bytes=VMEM_BYTES
        ),
        name="sum_gradients",
    )(*[g.reshape(FULL[name]) for g, name in zip(grads, MATS)], small)
    return outs, small_sum


def dot_nt(left, right):
    return lax.dot_general(
        left, right, (((1,), (1,)), ((), ())), preferred_element_type=jnp.float32
    )


def dot_nn(left, right):
    return jnp.dot(left, right, preferred_element_type=jnp.float32)


def dot_tn(left, right):
    return lax.dot_general(
        left, right, (((0,), (0,)), ((), ())), preferred_element_type=jnp.float32
    )


def feed_forward_kernel(ns_ref, nst_ref, g_ref, wg_ref, wu_ref, wd_ref, dg_ref, du_ref, dd_ref, out_ref, gs_ref):
    @pl.when(pl.program_id(0) == 0)
    def _():
        out_ref[...] = jnp.zeros_like(out_ref)
        gs_ref[...] = jnp.zeros_like(gs_ref)

    ns = ns_ref[...]
    wg = wg_ref[0]
    wu = wu_ref[0]
    gate_pre = dot_nn(ns, wg)
    up_pre = dot_nn(ns, wu)
    grad_hidden = dot_nt(g_ref[:, 0:256], wd_ref[0])
    for q in range(1, 4):
        grad_hidden += dot_nt(g_ref[:, 256 * q : 256 * q + 256], wd_ref[q])
    sig = jax.nn.sigmoid(gate_pre)
    silu = gate_pre * sig
    hidden = (silu * up_pre).astype(jnp.bfloat16)
    grad_gate = (grad_hidden * up_pre * sig * (1.0 + gate_pre * (1.0 - sig))).astype(jnp.bfloat16)
    grad_up = (grad_hidden * silu).astype(jnp.bfloat16)
    gs_ref[...] += dot_nt(grad_gate, wg) + dot_nt(grad_up, wu)
    nst = nst_ref[...]
    dg_ref[0] = dot_nn(nst, grad_gate).astype(jnp.bfloat16)
    du_ref[0] = dot_nn(nst, grad_up).astype(jnp.bfloat16)
    for q in range(4):
        cols = slice(256 * q, 256 * q + 256)
        out_ref[:, cols] += dot_nn(hidden, wd_ref[q])
        dd_ref[q] = dot_tn(hidden, g_ref[:, cols]).astype(jnp.bfloat16)


def feed_forward(ns, g, wg, wu, wd):
    whole = lambda shape: pl.BlockSpec(shape, lambda j: (0,) * len(shape))
    col = pl.BlockSpec((1, 1024, 384), lambda j: (j, 0, 0))
    row = pl.BlockSpec((4, 384, 256), lambda j: (0, j, 0))
    wide = jax.ShapeDtypeStruct((12, 1024, 384), jnp.bfloat16)
    return pl.pallas_call(
        feed_forward_kernel,
        grid=(12,),
        in_specs=[whole((256, 1024)), whole((1024, 256)), whole((256, 1024)), col, col, row],
        out_specs=[col, col, row, whole((256, 1024)), whole((256, 1024))],
        out_shape=[
            wide,
            wide,
            jax.ShapeDtypeStruct((4, 4608, 256), jnp.bfloat16),
            jax.ShapeDtypeStruct((256, 1024), jnp.float32),
            jax.ShapeDtypeStruct((256, 1024), jnp.float32),
        ],
        compiler_params=pltpu.CompilerParams(vmem_limit_bytes=VMEM_BYTES),
        name="feed_forward",
    )(ns, ns.T, g, wg, wu, wd)


def norm_back(grad_normed, field, scale, gain):
    normed = field * scale
    weighted = grad_normed * gain
    grad_field = scale * (weighted - normed * jnp.mean(weighted * normed, axis=-1, keepdims=True))
    return (grad_field, jnp.sum(grad_normed * normed, axis=0))


def adam_update(weight, first, second, gradient, step_rate, decay_rate):
    first_new = beta_one * first + (1.0 - beta_one) * gradient
    second_new = beta_two * second + (1.0 - beta_two) * gradient * gradient
    corrected = (
        first_new
        / (1.0 - beta_one**STEP)
        / (jnp.sqrt(second_new / (1.0 - beta_two**STEP)) + adam_eps)
    )
    return (weight - step_rate * (corrected + decay_rate * weight), first_new, second_new)


def from_behind(value, axis, steps):
    count = lax.axis_size(axis)
    leading, last = (max(0, -steps), min(count, count - steps))
    return lax.ppermute(value, axis, [(source, source + steps) for source in range(leading, last)])


def body(
    block_input,
    cotangent,
    in_weight,
    out_weight,
    gate_weight,
    up_weight,
    down_weight,
    small_params,
    in_first,
    out_first,
    gate_first,
    up_first,
    down_first,
    small_first,
    in_second,
    out_second,
    gate_second,
    up_second,
    down_second,
    small_second,
):
    position = lax.axis_index("fsdp")
    keep_tail = (position != 0).astype(jnp.float32)
    keep_head = (position != 31).astype(jnp.float32)
    full, small_low = gather(
        (in_weight, out_weight, gate_weight, up_weight, down_weight), small_params
    )
    w_in = full[0].reshape(12, 1024, 256)
    w_out = full[1].reshape(4, 1024, 256)
    w_gate = full[2].reshape(12, 1024, 384)
    w_up = full[3].reshape(12, 1024, 384)
    w_down = full[4].reshape(4, 4608, 256)
    conv_taps = small_low[0:KW]
    gain_first = small_low[KW]
    gain_second = small_low[KW + 1]

    rows = block_input.shape[1]
    tokens = block_input.astype(jnp.float32).reshape(256, 1024)
    scale_first = lax.rsqrt(jnp.mean(tokens * tokens, axis=-1, keepdims=True) + norm_eps)
    normed_first = (tokens * scale_first * gain_first).astype(jnp.bfloat16)
    projected = jnp.einsum("tk,pkn->tpn", normed_first, w_in, preferred_element_type=jnp.float32)
    projected = projected.reshape(256, 3072)
    gate_b = projected[:, 0:1024]
    gate_c = projected[:, 1024:2048]
    values = projected[:, 2048:3072]
    mixed_in = (gate_b * values).astype(jnp.bfloat16).reshape(MICRO, rows, 1024)
    tail_rows = from_behind(mixed_in[:, rows - (KW - 1) :], "fsdp", 1)
    extended = jnp.concatenate(
        [tail_rows.astype(jnp.float32) * keep_tail, mixed_in.astype(jnp.float32)], axis=1
    )
    conv_out = jnp.zeros((MICRO, rows, 1024), jnp.float32)
    for offset in range(KW):
        start = KW - 1 - offset
        conv_out = conv_out + conv_taps[offset] * extended[:, start : start + rows]
    conv_out = conv_out.reshape(256, 1024)
    gated_out = (gate_c * conv_out).astype(jnp.bfloat16)
    branch = jnp.einsum("tk,qkn->tqn", gated_out, w_out, preferred_element_type=jnp.float32)
    middle = tokens + branch.reshape(256, 1024)
    scale_second = lax.rsqrt(jnp.mean(middle * middle, axis=-1, keepdims=True) + norm_eps)
    normed_second = (middle * scale_second * gain_second).astype(jnp.bfloat16)

    grad_out = cotangent.reshape(256, 1024)
    grad_gate_weight, grad_up_weight, grad_down, ff_out, grad_second = feed_forward(
        normed_second, grad_out, w_gate, w_up, w_down
    )
    block_out = (middle + ff_out).astype(jnp.bfloat16)
    grad_middle_norm, grad_gain_second = norm_back(grad_second, middle, scale_second, gain_second)
    grad_middle = grad_out.astype(jnp.float32) + grad_middle_norm
    grad_branch = grad_middle.astype(jnp.bfloat16)
    grad_branch_cut = grad_branch.reshape(256, 4, 1024 // 4)
    grad_out_weight = jnp.einsum(
        "tk,tqn->qkn", gated_out, grad_branch_cut, preferred_element_type=jnp.float32
    )
    grad_gated = jnp.einsum(
        "tqn,qkn->tk", grad_branch_cut, w_out, preferred_element_type=jnp.float32
    )
    grad_c = grad_gated * conv_out
    grad_conv = (grad_gated * gate_c).astype(jnp.bfloat16).reshape(MICRO, rows, 1024)
    head_rows = from_behind(grad_conv[:, 0 : KW - 1], "fsdp", -1)
    conv_wide = grad_conv.astype(jnp.float32)
    grad_extended = jnp.concatenate([conv_wide, head_rows.astype(jnp.float32) * keep_head], axis=1)
    grad_mixed = jnp.zeros((MICRO, rows, 1024), jnp.float32)
    tap_grads = []
    for offset in range(KW):
        start = KW - 1 - offset
        grad_mixed = grad_mixed + conv_taps[offset] * grad_extended[:, offset : offset + rows]
        tap_grads.append(jnp.sum(conv_wide * extended[:, start : start + rows], axis=(0, 1)))
    grad_mixed = grad_mixed.reshape(256, 1024)
    grad_projected = jnp.concatenate(
        [grad_mixed * values, grad_c, grad_mixed * gate_b], axis=1
    ).astype(jnp.bfloat16)
    grad_projected_cut = grad_projected.reshape(256, 12, 256)
    grad_in_weight = jnp.einsum(
        "tk,tpn->pkn", normed_first, grad_projected_cut, preferred_element_type=jnp.float32
    )
    grad_first = jnp.einsum(
        "tpn,pkn->tk", grad_projected_cut, w_in, preferred_element_type=jnp.float32
    )
    grad_first_norm, grad_gain_first = norm_back(grad_first, tokens, scale_first, gain_first)
    input_grad = grad_middle + grad_first_norm
    zero_row = jnp.zeros_like(grad_gain_first)
    grad_small = jnp.stack(tap_grads + [grad_gain_first, grad_gain_second] + [zero_row] * 3)

    summed, small_sum = sums(
        (
            grad_in_weight.astype(jnp.bfloat16),
            grad_out_weight.astype(jnp.bfloat16),
            grad_gate_weight,
            grad_up_weight,
            grad_down,
        ),
        grad_small,
    )
    summed = [joined(g, name).astype(jnp.float32) for g, name in zip(summed, MATS)]
    small_mine = lax.dynamic_slice(small_sum, (0, position * 32), (5, 32))
    new_in = adam_update(in_weight, in_first, in_second, summed[0], rate_matrix, weight_decay)
    new_out = adam_update(out_weight, out_first, out_second, summed[1], rate_matrix, weight_decay)
    new_gate = adam_update(
        gate_weight, gate_first, gate_second, summed[2], rate_matrix, weight_decay
    )
    new_up = adam_update(up_weight, up_first, up_second, summed[3], rate_matrix, weight_decay)
    new_down = adam_update(
        down_weight, down_first, down_second, summed[4], rate_matrix, weight_decay
    )
    new_small = adam_update(small_params, small_first, small_second, small_mine, rate_small, 0.0)
    news = (new_in, new_out, new_gate, new_up, new_down, new_small)
    return (
        block_out.reshape(MICRO, rows, 1024),
        input_grad.reshape(MICRO, rows, 1024),
        *[n[0] for n in news],
        *[n[1] for n in news],
        *[n[2] for n in news],
    )


def solution(mesh):
    acts = P(None, ("dp", "fsdp"), None)
    params = (P("fsdp", None),) * 5 + (P(None, "fsdp"),)
    return jax.shard_map(
        body,
        mesh=mesh,
        in_specs=(acts, acts) + params * 3,
        out_specs=(acts, acts) + params * 3,
        check_vma=False,
    )
```

```python
import functools

import jax
import jax.numpy as jnp
from jax import lax
from jax.experimental import pallas as pl
from jax.experimental.pallas import tpu as pltpu
from jax.sharding import PartitionSpec as P

MESH = pl.DeviceIdType.MESH
KW = 3
MICRO = 2
STEP = 10

norm_eps = 1e-05
beta_one = 0.9
beta_two = 0.95
adam_eps = 1e-08
rate_matrix = 0.02
rate_small = 0.4
weight_decay = 0.1

MATS = ("in", "out", "gate", "up", "down")
THIRDS = {"in": 3, "out": 2, "gate": 3, "up": 3, "down": 3}
FULL = {
    "in": (3, 4, 4, 4, 2, 32, 256),
    "out": (4, 4, 4, 2, 2, 16, 256),
    "gate": (9, 4, 4, 4, 2, 32, 128),
    "up": (9, 4, 4, 4, 2, 32, 128),
    "down": (4, 4, 4, 2, 3, 48, 256),
}
OWN = {
    "in": (3, 4, 32, 256),
    "out": (4, 2, 16, 256),
    "gate": (9, 4, 32, 128),
    "up": (9, 4, 32, 128),
    "down": (4, 3, 48, 256),
}
BLOCK = {"in": (32, 256), "out": (16, 256), "gate": (32, 128), "up": (32, 128), "down": (48, 256)}
BY_THIRD = ("in", "gate", "up")
GATHER_ORDER = {0: ("z", "x"), 1: ("x", "y", "z"), 2: ("z", "x", "y")}
SUM_ORDER = {0: ("x", "z", "y"), 1: ("z", "y", "x"), 2: ("y", "x", "z")}
ALL = slice(None)
VMEM_BYTES = 63 * 1024 * 1024
FF_BLOCKS = 9


def coords():
    y = lax.axis_index("dp")
    f = lax.axis_index("fsdp")
    return {"y": y, "z": f // 8, "x": (f // 2) % 4, "c": f % 2}


def device(at):
    return (at["y"], at["z"] * 8 + at["x"] * 2 + at["c"])


def shifted(at, axis, by):
    new = dict(at)
    new[axis] = (at[axis] + by) % (2 if axis == "c" else 4)
    return new


def along(me, by):
    f = (me["z"] * 8 + me["x"] * 2 + me["c"] + by) % 32
    return {"y": me["y"], "z": f // 8, "x": (f // 2) % 4, "c": f % 2}


def meet(me):
    sem = pltpu.get_barrier_semaphore()
    peers = [shifted(me, "c", 1)] + [shifted(me, a, s) for a in "xyz" for s in (1, 2, 3)]
    peers += [along(me, 1), along(me, 31)]
    for p in peers:
        pl.semaphore_signal(sem, inc=1, device_id=device(p), device_id_type=MESH)
    pl.semaphore_wait(sem, len(peers))


def half_of(name, half):
    if name in BY_THIRD:
        return (ALL if half is None else pl.ds(16 * half, 16), ALL)
    return (ALL, ALL if half is None else pl.ds(128 * half, 128))


def view(ref, name, t, at, half=None):
    tail = half_of(name, half)
    if name in BY_THIRD:
        return ref.at[(t, at["y"], at["z"], at["x"], at["c"]) + tail]
    return ref.at[(at["y"], at["z"], at["x"], at["c"], t) + tail]


def own_view(ref, name, t, q=ALL):
    if name in BY_THIRD:
        return ref.at[t, q]
    return ref.at[q, t]


class Copy:
    def __init__(self, links, index, ends, target):
        self.links, self.index, self.ends, self.target = links, index, ends, target

    def descriptor(self):
        src, dst = self.ends()
        return pltpu.make_async_remote_copy(
            src,
            dst,
            self.links.send_sem.at[self.index],
            self.links.recv_sem.at[self.index],
            device_id=device(self.target()),
            device_id_type=MESH,
        )

    def wait_recv(self):
        self.descriptor().wait_recv()

    def wait_send(self):
        self.descriptor().wait_send()


class Links:
    def __init__(self, me, send_sem, recv_sem):
        self.me, self.send_sem, self.recv_sem = me, send_sem, recv_sem
        self.sent = []
        self.done = set()

    def send(self, ends, axis, by):
        return self.send_to(ends, lambda: shifted(self.me, axis, by))

    def send_to(self, ends, target):
        cp = Copy(self, len(self.sent), ends, target)
        cp.descriptor().start()
        self.sent.append(cp)
        return cp

    def left(self, cp):
        cp.wait_send()
        self.done.add(id(cp))

    def finish(self):
        for cp in self.sent:
            if id(cp) not in self.done:
                cp.wait_send()


def dot_nt(left, right):
    return lax.dot_general(
        left, right, (((1,), (1,)), ((), ())), preferred_element_type=jnp.float32
    )


def dot_nn(left, right):
    return jnp.dot(left, right, preferred_element_type=jnp.float32)


def norm_scale(field):
    return lax.rsqrt(jnp.mean(field * field, axis=-1, keepdims=True) + norm_eps)


def third(name, t):
    return pl.ds(3 * t, 3) if name in ("gate", "up") else t


def own_spots(name):
    rows, cols = BLOCK[name]
    if name in BY_THIRD:
        return [
            ((t, q), slice(0, rows), slice((4 * t + q) * cols, (4 * t + q + 1) * cols))
            for t in range(OWN[name][0])
            for q in range(4)
        ]
    return [
        ((q, t), slice(t * rows, (t + 1) * rows), slice(q * cols, (q + 1) * cols))
        for q in range(4)
        for t in range(OWN[name][1])
    ]


def forward_kernel(*refs):
    refs = list(refs)
    take = lambda n: [refs.pop(0) for _ in range(n)]
    weights = dict(zip(MATS, take(5)))
    small_own, block_in = take(2)
    outputs = dict(zip(MATS, take(5)))
    small_low, ns_out, nst_out, middle_out, gates_out, taps_out, nft_out, got_out = take(8)
    own = dict(zip(MATS, take(5)))
    in_full, out_full, small_full = take(3)
    ns, nst, middle, gates, taps, nft, got, normed, gate_c, ext, halo_out, halo_in = take(12)
    local_sem, send_sem, recv_sem = take(3)
    full = dict(outputs, **{"in": in_full, "out": out_full})
    me = coords()
    links = Links(me, send_sem, recv_sem)
    units = [(name, t) for name in MATS for t in range(THIRDS[name])]

    copies = []

    def copy(src, dst):
        cp = pltpu.make_async_copy(src, dst, local_sem.at[len(copies)])
        cp.start()
        copies.append(cp)

    for name in MATS:
        for spot, rows, cols in own_spots(name):
            own[name][spot] = weights[name][rows, cols].astype(jnp.bfloat16)
    small_full[me["z"], me["x"], me["c"]] = small_own[...]
    for name, t in units:
        q = ALL if t == 0 else me["y"]
        piece = third(name, t)
        copy(own_view(own[name], name, piece, q), view(full[name], name, piece, dict(me, y=q)))
    meet(me)
    for cp in copies:
        cp.wait()
    placed = len(copies)

    def send(u, at, axis, by, half=None):
        piece = view(full[u[0]], u[0], third(*u), at, half)
        return links.send(lambda: (piece, piece), axis, by)

    at_of = {u: dict(me, y=ALL) if u[1] == 0 else dict(me) for u in units}
    pending = {}
    swaps = {u: [] for u in units}

    def advance(u, step):
        order = GATHER_ORDER[u[1]]
        skipped = 3 - len(order)
        if step < 2 * skipped:
            return
        if step > 2 * skipped and step % 2 == 0:
            for cp in pending[u]:
                cp.wait_recv()
            done = order[step // 2 - 1 - skipped]
            if step == 6:
                swaps[u].append(send(u, shifted(at_of[u], done, 2), "c", 1))
                return
            at_of[u] = dict(at_of[u], **{done: ALL})
        axis = order[step // 2 - skipped]
        at = at_of[u]
        if step % 2 == 0:
            pending[u] = [send(u, at, axis, 1), send(u, at, axis, 3)]
            if step == 4:
                swaps[u].append(send(u, at, "c", 1))
            return
        sends = []
        for side, by in enumerate((1, 3)):
            pending[u][side].wait_recv()
            came = shifted(at, axis, 4 - by)
            sends.append(send(u, came, axis, by, side))
            if step == 5:
                swaps[u].append(send(u, came, "c", 1))
        pending[u] = sends

    groups = {"A": [u for u in units if u[0] in ("in", "out")]}
    groups.update({k: [u for u in units if u[0] == n] for k, n in (("G", "gate"), ("U", "up"), ("D", "down"))})

    def run(plan):
        for item in plan.split():
            for u in groups[item[0]]:
                advance(u, int(item[1]))

    small_at = [dict(me)]
    small_cps = []

    def small_step(axis):
        for cp in small_cps:
            cp.wait_recv()
        if small_cps:
            small_at[0] = dict(small_at[0], **{"z" if axis == "x" else "x": ALL})
        at = small_at[0]
        piece = small_full.at[at["z"], at["x"], at["c"]]
        steps = (1,) if axis == "c" else (1, 2, 3)
        small_cps[:] = [links.send(lambda: (piece, piece), axis, s) for s in steps]

    small_step("z")
    run("A0 G0 U0 D0 A1 G1 U1 D1")
    small_step("x")
    run("A2 G2 U2 D2 A3 G3 U3 D3")
    small_step("c")
    run("A4 G4 A5 U4 D4")

    for cp in small_cps:
        cp.wait_recv()
    for k in range(8):
        z, x = k // 2, 2 * (k % 2)
        small_low[:, 128 * k : 128 * k + 128] = (
            small_full[z, x, 0] + small_full[z, x, 1] + small_full[z, x + 1, 0] + small_full[z, x + 1, 1]
        )
    tokens = block_in[...].astype(jnp.float32)
    low = (tokens * norm_scale(tokens) * small_low[3:4]).astype(jnp.bfloat16)
    normed[...] = low
    nft[...] = low.T
    copy(nft, nft_out)
    run("A6")
    for u in groups["A"]:
        for cp in swaps[u]:
            cp.wait_recv()

    def conv_work():
        for q in range(4):
            cols = slice(256 * q, 256 * q + 256)
            cuts = []
            for t in range(3):
                weight = in_full[t, q].reshape(1024, 256)
                cuts.append(dot_nn(normed[...], weight))
            gate_c[:, cols] = cuts[1]
            for t in range(3):
                gates[t, :, cols] = cuts[t].astype(jnp.bfloat16)
            mixed = (cuts[0] * cuts[2]).astype(jnp.bfloat16)
            for m in range(MICRO):
                halo_out[m, :, cols] = mixed[128 * m + 112 : 128 * m + 128]
                ext[m, 8:136, cols] = mixed[128 * m : 128 * m + 128].astype(jnp.float32)
            yield
        sent = links.send_to(lambda: (halo_out, halo_in), lambda: along(me, 1))
        copy(in_full, outputs["in"])
        copy(out_full, outputs["out"])
        yield
        sent.wait_recv()
        keep = (me["z"] * 8 + me["x"] * 2 + me["c"] != 0).astype(jnp.float32)
        for m in range(MICRO):
            ext[m, 0:8] = halo_in[m].astype(jnp.float32)[8:16] * keep
        for m in range(MICRO):
            rows = slice(128 * m, 128 * m + 128)
            conv = small_low[0:1] * ext[m, 8:136]
            for k in range(1, KW):
                conv += small_low[k : k + 1] * ext[m, 8 - k : 136 - k]
            for k in range(KW):
                taps[k, rows] = ext[m, 8 - k : 136 - k].astype(jnp.bfloat16)
            gates[3, rows] = conv.astype(jnp.bfloat16)
            normed[rows] = (gate_c[rows] * conv).astype(jnp.bfloat16)
            yield
        copy(gates, gates_out)
        copy(taps, taps_out)
        got[...] = normed[...].T
        copy(got, got_out)
        yield
        for q in range(4):
            cols = slice(256 * q, 256 * q + 256)
            weight = out_full[q].reshape(1024, 256)
            middle[:, cols] = block_in[:, cols].astype(jnp.float32) + dot_nn(normed[...], weight)
        copy(middle, middle_out)
        yield
        field = middle[...]
        ns[...] = (field * norm_scale(field) * small_low[4:5]).astype(jnp.bfloat16)
        copy(ns, ns_out)
        nst[...] = ns[...].T
        copy(nst, nst_out)
        yield

    work = conv_work()
    for step in (5, 6):
        for key in "GUD":
            for u in groups[key]:
                next(work, None)
                advance(u, step)
    for _ in work:
        pass
    for key in "GUD":
        for u in groups[key]:
            for cp in swaps[u]:
                cp.wait_recv()
    for cp in copies[placed:]:
        cp.wait()
    links.finish()


def forward(weights, small, block_in):
    small_rows = jnp.pad(small.astype(jnp.bfloat16).astype(jnp.float32), ((0, 3), (0, 0)))
    lane = lax.broadcasted_iota(jnp.int32, (8, 128), 1) // 32
    small_own = jnp.where(lane == lax.axis_index("fsdp") % 4, jnp.tile(small_rows, (1, 4)), 0.0)
    in_vmem = pl.BlockSpec(memory_space=pltpu.VMEM)
    anywhere = pl.BlockSpec(memory_space=pl.ANY)
    bf16, f32 = jnp.bfloat16, jnp.float32
    kept = [
        ((256, 1024), bf16),
        ((1024, 256), bf16),
        ((256, 1024), f32),
        ((4, 256, 1024), bf16),
        ((3, 256, 1024), bf16),
        ((1024, 256), bf16),
        ((1024, 256), bf16),
    ]
    outs = pl.pallas_call(
        forward_kernel,
        out_shape=[jax.ShapeDtypeStruct(FULL[name], bf16) for name in MATS]
        + [jax.ShapeDtypeStruct((8, 1024), f32)]
        + [jax.ShapeDtypeStruct(*k) for k in kept],
        in_specs=[in_vmem] * 7,
        out_specs=[anywhere] * 5 + [in_vmem] + [anywhere] * 7,
        scratch_shapes=[pltpu.VMEM(OWN[name], bf16) for name in MATS]
        + [pltpu.VMEM(FULL["in"], bf16), pltpu.VMEM(FULL["out"], bf16)]
        + [pltpu.VMEM((4, 4, 2, 8, 128), f32)]
        + [pltpu.VMEM(*k) for k in kept]
        + [
            pltpu.VMEM((256, 1024), bf16),
            pltpu.VMEM((256, 1024), f32),
            pltpu.VMEM((2, 136, 1024), f32),
            pltpu.VMEM((2, 16, 1024), bf16),
            pltpu.VMEM((2, 16, 1024), bf16),
            pltpu.SemaphoreType.DMA((32,)),
            pltpu.SemaphoreType.DMA((256,)),
            pltpu.SemaphoreType.DMA((256,)),
        ],
        compiler_params=pltpu.CompilerParams(
            collective_id=1, has_side_effects=True, vmem_limit_bytes=VMEM_BYTES
        ),
        name="forward",
    )(*weights, small_own, block_in)
    return outs[0:5], outs[5:]


def norm_back(grad_normed, field, gain):
    scale = norm_scale(field)
    normed = field * scale
    weighted = grad_normed * gain
    grad_field = scale * (weighted - normed * jnp.mean(weighted * normed, axis=-1, keepdims=True))
    return (grad_field, jnp.sum(grad_normed * normed, axis=0, keepdims=True))


def order_of(name, t):
    if name == "gate":
        return SUM_ORDER[(2 * t) % 3]
    if name == "up":
        return SUM_ORDER[(2 * t + 1) % 3]
    return SUM_ORDER[t]


def rest_axes(unit, p):
    return [a for a in "yzx" if a in order_of(*unit)[p + 1 :]]


BATCHES = [[("gate", j), ("up", j)] for j in range(FF_BLOCKS)]
BATCHES += [[("down", t) for t in range(3)], [("out", 0), ("out", 1)], [("in", t) for t in range(3)]]
UNITS = [u for batch in BATCHES for u in batch]


def landing(unit):
    rows, cols = BLOCK[unit[0]]
    half = (rows // 2, cols) if unit[0] in BY_THIRD else (rows, cols // 2)
    shapes = []
    for p in range(3):
        lead = (2,) + (4,) * len(rest_axes(unit, p))
        shapes.append((lead + half, lead + (rows, cols)))
    return shapes


def part(ref, unit, at, half=None):
    name, t = unit
    tail = half_of(name, half)
    if name in BY_THIRD:
        return ref.at[(t, at["y"], at["z"], at["x"]) + tail]
    return ref.at[(at["y"], at["z"], at["x"], t) + tail]


def lanes(unit):
    k = UNITS.index(unit)
    return (k % 2,) if k < 2 * FF_BLOCKS else (0, 1)


def cut(ref, unit):
    rows, cols = BLOCK[unit[0]]
    return ref.at[:, :, :, pl.ds(0, rows), pl.ds(128 * lanes(unit)[0], cols)]


EVERY = {"y": ALL, "z": ALL, "x": ALL}


class Sums:
    def __init__(self, me, links, mine, theirs, outs, staging, slots, slot_sem, land):
        self.me, self.links = me, links
        self.mine, self.theirs, self.outs = mine, theirs, outs
        self.staging, self.slots, self.slot_sem, self.land = staging, slots, slot_sem, land
        self.at = {u: dict(EVERY) for u in UNITS}
        self.swaps, self.loads, self.pending, self.last = {}, {}, {}, []
        self.users = {}

    def slot_of(self, unit):
        k = UNITS.index(unit)
        return (k // 2) % 2 if k < 2 * FF_BLOCKS else k % 2

    def room(self, unit):
        for lane in lanes(unit):
            user = self.users.get((self.slot_of(unit), lane))
            if user is not None and id(user) not in self.links.done:
                self.links.left(user)
        return cut(self.staging.at[self.slot_of(unit)], unit)

    def swap(self, unit):
        slot = self.slot_of(unit)

        def ends():
            return cut(self.staging.at[slot], unit), part(self.theirs[unit[0]], unit, EVERY)

        self.swaps[unit] = self.links.send(ends, "c", 1)
        for lane in lanes(unit):
            self.users[slot, lane] = self.swaps[unit]

    def load(self, unit):
        k = UNITS.index(unit)
        self.swaps[unit].wait_recv()
        src = part(self.theirs[unit[0]], unit, EVERY)
        cp = pltpu.make_async_copy(src, cut(self.slots, unit), self.slot_sem.at[k])
        cp.start()
        self.loads[unit] = cp

    def join(self, unit):
        self.loads[unit].wait()
        slot = cut(self.slots, unit)
        total = part(self.mine[unit[0]], unit, EVERY)

        def step(i, carry):
            spot = (i // 4, i % 4)
            total[spot] = total[spot] + slot[spot]
            return carry

        lax.fori_loop(0, 16, step, 0, unroll=2)
        self.start(unit, 0)

    def add(self, unit, p, at, half, *landed):
        rest = rest_axes(unit, p)
        if len(rest) < 2:
            ref = part(self.mine[unit[0]], unit, at, half)
            self.add_block(ref, *[r[...] for r in landed])
            return

        def step(i, carry):
            ref = part(self.mine[unit[0]], unit, dict(at, **{rest[0]: i}), half)
            self.add_block(ref, *[r[i] for r in landed])
            return carry

        lax.fori_loop(0, 4, step, 0, unroll=2)

    def add_block(self, ref, *values):
        if len(values) == 1:
            ref[...] = ref[...] + values[0]
            return
        total = ref[...].astype(jnp.float32)
        for value in values:
            total = total + value.astype(jnp.float32)
        ref[...] = total.astype(jnp.bfloat16)

    def spot(self, at, axis, by):
        return dict(at, **{axis: (self.me[axis] + by) % 4})

    def start(self, unit, p):
        axis = order_of(*unit)[p]
        at = self.at[unit]
        halves = self.land[unit][p][0]
        ref = self.mine[unit[0]]

        def ends(side):
            return lambda: (part(ref, unit, self.spot(at, axis, 2), side), halves.at[side])

        self.pending[unit] = [
            self.links.send(ends(0), axis, 1),
            self.links.send(ends(1), axis, 3),
        ]

    def middle(self, unit, p):
        axis = order_of(*unit)[p]
        at = self.at[unit]
        halves, blocks = self.land[unit][p]
        ref = self.mine[unit[0]]
        sends = []

        def ends(side, by):
            return lambda: (part(ref, unit, self.spot(at, axis, by)), blocks.at[side])

        for side, by in enumerate((1, 3)):
            self.pending[unit][side].wait_recv()
            self.add(unit, p, self.spot(at, axis, by), side, halves.at[side])
            sends.append(self.links.send(ends(side, by), axis, by))
        self.pending[unit] = sends

    def end(self, unit, p):
        axis = order_of(*unit)[p]
        blocks = self.land[unit][p][1]
        for cp in self.pending[unit]:
            cp.wait_recv()
        self.at[unit] = dict(self.at[unit], **{axis: self.me[axis]})
        self.add(unit, p, self.at[unit], None, blocks.at[0], blocks.at[1])
        if p < 2:
            self.start(unit, p + 1)
            return

        def mine_out():
            return own_view(self.outs[unit[0]], unit[0], unit[1], self.me["y"])

        mine_out()[...] = part(self.mine[unit[0]], unit, self.at[unit])[...]
        for by in (1, 2, 3):
            self.last.append(self.links.send(lambda: (mine_out(), mine_out()), "y", by))

    def stage(self, s, batch):
        for unit in batch:
            if s % 2 == 0:
                self.middle(unit, s // 2)
            else:
                self.end(unit, s // 2)


def backward_kernel(*refs):
    refs = list(refs)
    take = lambda n: [refs.pop(0) for _ in range(n)]
    ns, g, small_low = take(3)
    nst_hbm, wg, wu, wd, w_in, w_out = take(6)
    middle_hbm, tokens_hbm, gates_hbm, taps_hbm, nft_hbm, got_hbm = take(6)
    outs = dict(zip(MATS, take(5)))
    small_out, block_out, input_grad = take(3)
    theirs = dict(zip(MATS, take(5)))
    mine = dict(zip(MATS, take(5)))
    land = {u: [tuple(take(2)) for _ in range(3)] for u in UNITS}
    staging, slots, hidden_t, grad_ns, ff_out, nst = take(6)
    halo_out, halo_in, small_land = take(3)
    local_sem, slot_sem, send_sem, recv_sem = take(4)
    me = coords()
    links = Links(me, send_sem, recv_sem)
    sums = Sums(me, links, mine, theirs, outs, staging, slots, slot_sem, land)

    def first_loads(wg_s, wu_s, wd_s):
        def fetch(j):
            s = j % 2
            pairs = [
                (wg.at[j], wg_s.at[s]),
                (wu.at[j], wu_s.at[s]),
                (wd.at[:, pl.ds(512 * j, 512)], wd_s.at[s]),
            ]
            cps = [
                pltpu.make_async_copy(a, b, local_sem.at[3 * s + i]) for i, (a, b) in enumerate(pairs)
            ]
            for cp in cps:
                cp.start()
            return cps

        return fetch

    def drive(tick, work):
        tasks = []
        if 0 <= tick - 1 < len(BATCHES):
            batch = BATCHES[tick - 1]
            ahead = 2 if tick - 1 < FF_BLOCKS else 1
            for unit in batch[:ahead]:
                sums.load(unit)

            def joins():
                for i, unit in enumerate(batch):
                    if i >= ahead:
                        sums.load(unit)
                    sums.join(unit)

            tasks.append(joins)
        for s in range(6):
            if 0 <= tick - 2 - s < len(BATCHES):
                tasks.append(functools.partial(sums.stage, s, BATCHES[tick - 2 - s]))
        for _ in work if work is not None else ():
            for _ in range(2):
                if tasks:
                    tasks.pop(0)()
        for task in tasks:
            task()

    def spread(name, t, value, half):
        rows, cols = BLOCK[name]
        ref = part(mine[name], (name, t), EVERY) if half == 0 else sums.room((name, t))
        for q in range(4):
            piece = value[:, cols * q : cols * q + cols].astype(jnp.bfloat16)
            ref[q] = piece.reshape(4, 4, rows, cols)
        if half == 1:
            sums.swap((name, t))

    def ff_block(j, wg_s, wu_s, wd_s, fetch, fetched):
        for cp in fetched[j]:
            cp.wait()
        if j + 1 < FF_BLOCKS:
            fetched[j + 1] = fetch(j + 1)
        s = j % 2
        gate_w = jnp.concatenate([wg_s[s, q] for q in range(4)], axis=1)
        up_w = jnp.concatenate([wu_s[s, q] for q in range(4)], axis=1)
        gate_pre = dot_nn(ns[...], gate_w)
        up_pre = dot_nn(ns[...], up_w)
        grad_hidden = dot_nt(g[:, 0:256], wd_s[s, 0])
        for q in range(1, 4):
            grad_hidden += dot_nt(g[:, 256 * q : 256 * q + 256], wd_s[s, q])
        sig = jax.nn.sigmoid(gate_pre)
        silu = gate_pre * sig
        hidden = (silu * up_pre).astype(jnp.bfloat16)
        grad_gate = (grad_hidden * up_pre * sig * (1.0 + gate_pre * (1.0 - sig))).astype(
            jnp.bfloat16
        )
        grad_up = (grad_hidden * silu).astype(jnp.bfloat16)
        for half in (1, 0):
            spread("gate", j, dot_nn(nst[half].reshape(512, 256), grad_gate), half)
            spread("up", j, dot_nn(nst[half].reshape(512, 256), grad_up), half)
        yield
        turned = hidden.T
        for k in range(32):
            row = 512 * j + 16 * k
            f, r = row // 144, row % 144
            hidden_t[f // 2, f % 2, r : r + 16, :] = turned[16 * k : 16 * k + 16]
        fresh = dot_nt(grad_gate, gate_w) + dot_nt(grad_up, up_w)
        if j == 0:
            grad_ns[...] = fresh
        else:
            grad_ns[...] += fresh
        for q in range(4):
            cols = slice(256 * q, 256 * q + 256)
            if j == 0:
                ff_out[:, cols] = dot_nn(hidden, wd_s[s, q])
            else:
                ff_out[:, cols] += dot_nn(hidden, wd_s[s, q])
        yield

    def feed_forward(wg_s, wu_s, wd_s):
        fetch = first_loads(wg_s, wu_s, wd_s)
        by_core = [
            pltpu.make_async_copy(nst_hbm.at[:, (me["c"] + h) % 2], nst.at[h], local_sem.at[6 + h])
            for h in (0, 1)
        ]
        for cp in by_core:
            cp.start()
        fetched = {0: fetch(0)}
        meet(me)
        for cp in by_core:
            cp.wait()
        for j in range(FF_BLOCKS):
            drive(j, ff_block(j, wg_s, wu_s, wd_s, fetch, fetched))

    pl.run_scoped(
        feed_forward,
        pltpu.VMEM((2, 4, 1024, 128), jnp.bfloat16),
        pltpu.VMEM((2, 4, 1024, 128), jnp.bfloat16),
        pltpu.VMEM((2, 4, 512, 256), jnp.bfloat16),
    )

    def give_input_grad():
        return pltpu.make_async_copy(ff_out, input_grad, local_sem.at[15])

    small_at = [0]
    small_cps = []

    def small_send(axis):
        steps = (1,) if axis == "c" else (1, 2, 3)
        first = small_at[0]
        small_at[0] += len(steps)
        small_cps[:] = [
            links.send(lambda s=s: (small_out, small_land.at[first + s - 1]), axis, s)
            for s in steps
        ]

    def small_take():
        first = small_at[0] - len(small_cps)
        for cp in small_cps:
            cp.wait_recv()
        for cp in small_cps:
            links.left(cp)
        total = small_out[...]
        for s in range(len(small_cps)):
            total = total + small_land[first + s]
        small_out[...] = total

    def conv_branch(middle, tokens, gates, taps_in, nft, got, wi_s, conv_ext, grad_proj):
        wo_s, grad_in = wi_s.at[1], ff_out
        sources = [middle_hbm, tokens_hbm, gates_hbm, taps_hbm, w_out]
        places = [middle, tokens, gates, taps_in, wo_s]
        for h in (0, 1):
            sources += [nft_hbm.at[:, (me["c"] + h) % 2], got_hbm.at[:, (me["c"] + h) % 2]]
            places += [nft.at[h], got.at[h]]
        cps = [pltpu.make_async_copy(a, b, local_sem.at[i]) for i, (a, b) in enumerate(zip(sources, places))]
        for cp in cps:
            cp.start()
        fetched = {}

        def fetch(t):
            fetched[t] = pltpu.make_async_copy(
                w_in.at[pl.ds(4 * t, 4)], wi_s.at[t % 2], local_sem.at[10 + t]
            )
            fetched[t].start()

        fetch(0)

        def down_work():
            for t in range(3):
                for half in (1, 0):
                    c = (me["c"] + half) % 2
                    left = hidden_t[:, c, 48 * t : 48 * t + 48, :].reshape(768, 256)
                    spread("down", t, dot_nn(left, g[...]), half)
                yield

        drive(9, down_work())
        for cp in cps:
            cp.wait()

        def out_work():
            gain_second = small_low[4:5]
            block_out[...] = (middle[...] + ff_out[...]).astype(jnp.bfloat16)
            grad_norm, grad_gain = norm_back(grad_ns[...], middle[...], gain_second)
            small_out[4:5] = grad_gain
            grad_middle = g[...].astype(jnp.float32) + grad_norm
            middle[...] = grad_middle
            grad_branch = grad_middle.astype(jnp.bfloat16)
            for half in (1, 0):
                whole = dot_nn(got[half].reshape(512, 256), grad_branch).reshape(16, 2, 16, 1024)
                for t in range(2):
                    spread("out", t, whole[:, t].reshape(256, 1024), half)
            yield
            grad_gated = dot_nt(grad_branch[:, 0:256], wo_s[0])
            for q in range(1, 4):
                grad_gated += dot_nt(grad_branch[:, 256 * q : 256 * q + 256], wo_s[q])
            grad_conv = (grad_gated * gates[1].astype(jnp.float32)).astype(jnp.bfloat16)
            for m in range(MICRO):
                halo_out[m] = grad_conv[128 * m : 128 * m + 16]
            sent = links.send_to(lambda: (halo_out, halo_in), lambda: along(me, 31))
            grad_proj[:, 1024:2048] = (grad_gated * gates[3].astype(jnp.float32)).astype(jnp.bfloat16)
            wide = grad_conv.astype(jnp.float32)
            for m in range(MICRO):
                conv_ext[m, 0:128] = wide[128 * m : 128 * m + 128]
            for k in range(KW):
                small_out[k : k + 1] = jnp.sum(
                    wide * taps_in[k].astype(jnp.float32), axis=0, keepdims=True
                )
            yield
            sent.wait_recv()
            keep = (me["z"] * 8 + me["x"] * 2 + me["c"] != 31).astype(jnp.float32)
            for m in range(MICRO):
                conv_ext[m, 128:136] = halo_in[m].astype(jnp.float32)[0:8] * keep
            for m in range(MICRO):
                mixed = small_low[0:1] * conv_ext[m, 0:128]
                for k in range(1, KW):
                    mixed += small_low[k : k + 1] * conv_ext[m, k : k + 128]
                rows = slice(128 * m, 128 * m + 128)
                grad_proj[rows, 0:1024] = (mixed * gates[2, rows].astype(jnp.float32)).astype(
                    jnp.bfloat16
                )
                grad_proj[rows, 2048:3072] = (mixed * gates[0, rows].astype(jnp.float32)).astype(
                    jnp.bfloat16
                )

        drive(10, out_work())
        fetch(1)

        def in_work():
            for t in range(3):
                cols = slice(1024 * t, 1024 * t + 1024)
                for half in (1, 0):
                    spread("in", t, dot_nn(nft[half].reshape(512, 256), grad_proj[:, cols]), half)
                yield

        drive(11, in_work())

        def token_work():
            for t in range(3):
                fetched[t].wait()
                for q in range(4):
                    cols = slice(256 * (4 * t + q), 256 * (4 * t + q) + 256)
                    fresh = dot_nt(grad_proj[:, cols], wi_s[t % 2, q])
                    if t == 0 and q == 0:
                        grad_in[...] = fresh
                    else:
                        grad_in[...] += fresh
                if t == 0:
                    fetch(2)
                yield
            x = tokens[...].astype(jnp.float32)
            grad_norm, grad_gain = norm_back(grad_in[...], x, small_low[3:4])
            small_out[3:4] = grad_gain
            small_out[5:8] = jnp.zeros((3, 1024), jnp.float32)
            grad_in[...] = middle[...] + grad_norm
            give_input_grad().start()
            small_send("c")

        drive(12, token_work())

    pl.run_scoped(
        conv_branch,
        pltpu.VMEM((256, 1024), jnp.float32),
        pltpu.VMEM((256, 1024), jnp.bfloat16),
        pltpu.VMEM((4, 256, 1024), jnp.bfloat16),
        pltpu.VMEM((3, 256, 1024), jnp.bfloat16),
        pltpu.VMEM((2, 16, 32, 256), jnp.bfloat16),
        pltpu.VMEM((2, 16, 32, 256), jnp.bfloat16),
        pltpu.VMEM((2, 4, 1024, 256), jnp.bfloat16),
        pltpu.VMEM((2, 136, 1024), jnp.float32),
        pltpu.VMEM((256, 3072), jnp.bfloat16),
    )
    for i, axis in enumerate("xzy"):
        drive(13 + i, None)
        small_take()
        small_send(axis)
    drive(16, None)
    small_take()
    for tick in range(17, len(BATCHES) + 7):
        drive(tick, None)
    for cp in sums.last:
        cp.wait_recv()
    give_input_grad().wait()
    links.finish()


def backward(ns, g, small_low, nst, w_gate, w_up, w_down, w_in, w_out, middle, tokens, *rest):
    in_vmem = pl.BlockSpec(memory_space=pltpu.VMEM)
    anywhere = pl.BlockSpec(memory_space=pl.ANY)
    core_shape = {}
    for name in MATS:
        shape = list(FULL[name])
        del shape[4 if name in BY_THIRD else 3]
        core_shape[name] = tuple(shape)
    scratch = [pltpu.VMEM(core_shape[name], jnp.bfloat16) for name in MATS]
    for u in UNITS:
        for halves, blocks in landing(u):
            scratch += [pltpu.VMEM(halves, jnp.bfloat16), pltpu.VMEM(blocks, jnp.bfloat16)]
    scratch += [
        pltpu.VMEM((2, 4, 4, 4, 48, 256), jnp.bfloat16),
        pltpu.VMEM((4, 4, 4, 48, 256), jnp.bfloat16),
        pltpu.VMEM((16, 2, 144, 256), jnp.bfloat16),
        pltpu.VMEM((256, 1024), jnp.float32),
        pltpu.VMEM((256, 1024), jnp.float32),
        pltpu.VMEM((2, 16, 32, 256), jnp.bfloat16),
        pltpu.VMEM((2, 16, 1024), jnp.bfloat16),
        pltpu.VMEM((2, 16, 1024), jnp.bfloat16),
        pltpu.VMEM((10, 8, 1024), jnp.float32),
        pltpu.SemaphoreType.DMA((16,)),
        pltpu.SemaphoreType.DMA((len(UNITS),)),
        pltpu.SemaphoreType.DMA((480,)),
        pltpu.SemaphoreType.DMA((480,)),
    ]
    outs = pl.pallas_call(
        backward_kernel,
        out_shape=[jax.ShapeDtypeStruct(OWN[name], jnp.bfloat16) for name in MATS]
        + [
            jax.ShapeDtypeStruct((8, 1024), jnp.float32),
            jax.ShapeDtypeStruct((256, 1024), jnp.bfloat16),
            jax.ShapeDtypeStruct((256, 1024), jnp.float32),
        ]
        + [jax.ShapeDtypeStruct(core_shape[name], jnp.bfloat16) for name in MATS],
        in_specs=[in_vmem] * 3 + [anywhere] * 12,
        out_specs=[in_vmem] * 7 + [anywhere] * 6,
        scratch_shapes=scratch,
        compiler_params=pltpu.CompilerParams(
            collective_id=2, has_side_effects=True, vmem_limit_bytes=VMEM_BYTES
        ),
        name="backward",
    )(ns, g, small_low, nst, w_gate, w_up, w_down, w_in, w_out, middle, tokens, *rest)
    return outs[0:5], outs[5], outs[6], outs[7]


def adam_update(weight, first, second, gradient, step_rate, decay_rate):
    first_new = beta_one * first + (1.0 - beta_one) * gradient
    second_new = beta_two * second + (1.0 - beta_two) * gradient * gradient
    corrected = (
        first_new
        / (1.0 - beta_one**STEP)
        / (jnp.sqrt(second_new / (1.0 - beta_two**STEP)) + adam_eps)
    )
    return (weight - step_rate * (corrected + decay_rate * weight), first_new, second_new)


def adam_kernel(*refs):
    sources = [dict(zip(MATS, refs[5 * i : 5 * i + 5])) for i in range(4)]
    results = [dict(zip(MATS, refs[20 + 5 * i : 25 + 5 * i])) for i in range(3)]
    weights, firsts, seconds, sums = sources

    def update(name):
        rows, cols = BLOCK[name]
        shape = sums[name].shape
        for a in range(shape[0]):
            for b in range(shape[1]):
                if name in BY_THIRD:
                    spot = (slice(0, rows), slice((4 * a + b) * cols, (4 * a + b + 1) * cols))
                else:
                    spot = (slice(b * rows, (b + 1) * rows), slice(a * cols, (a + 1) * cols))
                new = adam_update(
                    weights[name][spot],
                    firsts[name][spot],
                    seconds[name][spot],
                    sums[name][a, b].astype(jnp.float32),
                    rate_matrix,
                    weight_decay,
                )
                for result, value in zip(results, new):
                    result[name][spot] = value

    for name in ("in", "gate", "up", "down"):
        update(name)

    @pl.when(pl.program_id(0) == 0)
    def _():
        update("out")


def adam(weights, firsts, seconds, sums):
    shard = {
        "in": pl.BlockSpec((32, 1024), lambda i: (0, i)),
        "out": pl.BlockSpec((32, 1024), lambda i: (0, 0)),
        "gate": pl.BlockSpec((32, 1536), lambda i: (0, i)),
        "up": pl.BlockSpec((32, 1536), lambda i: (0, i)),
        "down": pl.BlockSpec((48, 1024), lambda i: (i, 0)),
    }
    pieces = {
        "in": pl.BlockSpec((1, 4, 32, 256), lambda i: (i, 0, 0, 0)),
        "out": pl.BlockSpec((4, 2, 16, 256), lambda i: (0, 0, 0, 0)),
        "gate": pl.BlockSpec((3, 4, 32, 128), lambda i: (i, 0, 0, 0)),
        "up": pl.BlockSpec((3, 4, 32, 128), lambda i: (i, 0, 0, 0)),
        "down": pl.BlockSpec((4, 1, 48, 256), lambda i: (0, i, 0, 0)),
    }
    in_order = [shard[name] for name in MATS]
    outs = pl.pallas_call(
        adam_kernel,
        grid=(3,),
        in_specs=in_order * 3 + [pieces[name] for name in MATS],
        out_specs=in_order * 3,
        out_shape=[jax.ShapeDtypeStruct(w.shape, jnp.float32) for w in weights] * 3,
        compiler_params=pltpu.CompilerParams(vmem_limit_bytes=VMEM_BYTES),
        name="adam",
    )(*weights, *firsts, *seconds, *sums)
    return outs[0:5], outs[5:10], outs[10:15]


def body(
    block_input,
    cotangent,
    in_weight,
    out_weight,
    gate_weight,
    up_weight,
    down_weight,
    small_params,
    in_first,
    out_first,
    gate_first,
    up_first,
    down_first,
    small_first,
    in_second,
    out_second,
    gate_second,
    up_second,
    down_second,
    small_second,
):
    rows = block_input.shape[1]
    tokens = block_input.reshape(256, 1024)
    full, kept = forward(
        (in_weight, out_weight, gate_weight, up_weight, down_weight), small_params, tokens
    )
    small_low, ns, nst, middle, gates, taps, nft, got = kept
    cuts = (16, 2, 32, 256)
    summed, small_sum, block_out, input_grad = backward(
        ns,
        cotangent.reshape(256, 1024),
        small_low,
        nst.reshape(cuts),
        full[2].reshape(9, 4, 1024, 128),
        full[3].reshape(9, 4, 1024, 128),
        full[4].reshape(4, 4608, 256),
        full[0].reshape(12, 1024, 256),
        full[1].reshape(4, 1024, 256),
        middle,
        tokens,
        gates,
        taps,
        nft.reshape(cuts),
        got.reshape(cuts),
    )
    position = lax.axis_index("fsdp")
    small_mine = lax.dynamic_slice(small_sum, (0, position * 32), (5, 32))
    new_weights, new_firsts, new_seconds = adam(
        (in_weight, out_weight, gate_weight, up_weight, down_weight),
        (in_first, out_first, gate_first, up_first, down_first),
        (in_second, out_second, gate_second, up_second, down_second),
        summed,
    )
    new_small = adam_update(small_params, small_first, small_second, small_mine, rate_small, 0.0)
    return (
        block_out.reshape(MICRO, rows, 1024),
        input_grad.reshape(MICRO, rows, 1024),
        *new_weights,
        new_small[0],
        *new_firsts,
        new_small[1],
        *new_seconds,
        new_small[2],
    )


def solution(mesh):
    acts = P(None, ("dp", "fsdp"), None)
    params = (P("fsdp", None),) * 5 + (P(None, "fsdp"),)
    return jax.shard_map(
        body,
        mesh=mesh,
        in_specs=(acts, acts) + params * 3,
        out_specs=(acts, acts) + params * 3,
        check_vma=False,
    )
```

```python
import functools

import jax
import jax.numpy as jnp
from jax import lax
from jax.experimental import pallas as pl
from jax.experimental.pallas import tpu as pltpu
from jax.sharding import PartitionSpec as P

MESH = pl.DeviceIdType.MESH
KW = 3
MICRO = 2
STEP = 10

norm_eps = 1e-05
beta_one = 0.9
beta_two = 0.95
adam_eps = 1e-08
rate_matrix = 0.02
rate_small = 0.4
weight_decay = 0.1

MATS = ("in", "out", "gate", "up", "down")
THIRDS = {"in": 3, "out": 2, "gate": 3, "up": 3, "down": 3}
FULL = {
    "in": (3, 4, 4, 4, 2, 32, 256),
    "out": (4, 4, 4, 2, 2, 16, 256),
    "gate": (9, 4, 4, 4, 2, 32, 128),
    "up": (9, 4, 4, 4, 2, 32, 128),
    "down": (4, 4, 4, 2, 3, 48, 256),
}
OWN = {
    "in": (3, 4, 32, 256),
    "out": (4, 2, 16, 256),
    "gate": (9, 4, 32, 128),
    "up": (9, 4, 32, 128),
    "down": (4, 3, 48, 256),
}
BLOCK = {"in": (32, 256), "out": (16, 256), "gate": (32, 128), "up": (32, 128), "down": (48, 256)}
BY_THIRD = ("in", "gate", "up")
GATHER_ORDER = {0: ("z", "x"), 1: ("x", "y", "z"), 2: ("z", "x", "y")}
SUM_ORDER = {0: ("x", "z", "y"), 1: ("z", "y", "x"), 2: ("y", "x", "z")}
ALL = slice(None)
VMEM_BYTES = 63 * 1024 * 1024
FF_BLOCKS = 9


def coords():
    y = lax.axis_index("dp")
    f = lax.axis_index("fsdp")
    return {"y": y, "z": f // 8, "x": (f // 2) % 4, "c": f % 2}


def device(at):
    return (at["y"], at["z"] * 8 + at["x"] * 2 + at["c"])


def shifted(at, axis, by):
    new = dict(at)
    new[axis] = (at[axis] + by) % (2 if axis == "c" else 4)
    return new


def along(me, by):
    f = (me["z"] * 8 + me["x"] * 2 + me["c"] + by) % 32
    return {"y": me["y"], "z": f // 8, "x": (f // 2) % 4, "c": f % 2}


def meet(me):
    sem = pltpu.get_barrier_semaphore()
    peers = [shifted(me, "c", 1)] + [shifted(me, a, s) for a in "xyz" for s in (1, 2, 3)]
    peers += [along(me, 1), along(me, 31)]
    for p in peers:
        pl.semaphore_signal(sem, inc=1, device_id=device(p), device_id_type=MESH)
    pl.semaphore_wait(sem, len(peers))


def half_of(name, half):
    if name in BY_THIRD:
        return (ALL if half is None else pl.ds(16 * half, 16), ALL)
    return (ALL, ALL if half is None else pl.ds(128 * half, 128))


def view(ref, name, t, at, half=None):
    tail = half_of(name, half)
    if name in BY_THIRD:
        return ref.at[(t, at["y"], at["z"], at["x"], at["c"]) + tail]
    return ref.at[(at["y"], at["z"], at["x"], at["c"], t) + tail]


def own_view(ref, name, t, q=ALL):
    if name in BY_THIRD:
        return ref.at[t, q]
    return ref.at[q, t]


class Copy:
    def __init__(self, links, index, ends, target):
        self.links, self.index, self.ends, self.target = links, index, ends, target

    def descriptor(self):
        src, dst = self.ends()
        return pltpu.make_async_remote_copy(
            src,
            dst,
            self.links.send_sem.at[self.index],
            self.links.recv_sem.at[self.index],
            device_id=device(self.target()),
            device_id_type=MESH,
        )

    def wait_recv(self):
        self.descriptor().wait_recv()

    def wait_send(self):
        self.descriptor().wait_send()


class Links:
    def __init__(self, me, send_sem, recv_sem):
        self.me, self.send_sem, self.recv_sem = me, send_sem, recv_sem
        self.sent = []
        self.done = set()

    def send(self, ends, axis, by):
        return self.send_to(ends, lambda: shifted(self.me, axis, by))

    def send_to(self, ends, target):
        cp = Copy(self, len(self.sent), ends, target)
        cp.descriptor().start()
        self.sent.append(cp)
        return cp

    def left(self, cp):
        cp.wait_send()
        self.done.add(id(cp))

    def finish(self):
        for cp in self.sent:
            if id(cp) not in self.done:
                cp.wait_send()


def dot_nt(left, right):
    return lax.dot_general(
        left, right, (((1,), (1,)), ((), ())), preferred_element_type=jnp.float32
    )


def dot_nn(left, right):
    return jnp.dot(left, right, preferred_element_type=jnp.float32)


def norm_scale(field):
    return lax.rsqrt(jnp.mean(field * field, axis=-1, keepdims=True) + norm_eps)


def third(name, t):
    return pl.ds(3 * t, 3) if name in ("gate", "up") else t


def own_spots(name):
    rows, cols = BLOCK[name]
    if name in BY_THIRD:
        return [
            ((t, q), slice(0, rows), slice((4 * t + q) * cols, (4 * t + q + 1) * cols))
            for t in range(OWN[name][0])
            for q in range(4)
        ]
    return [
        ((q, t), slice(t * rows, (t + 1) * rows), slice(q * cols, (q + 1) * cols))
        for q in range(4)
        for t in range(OWN[name][1])
    ]


def forward_kernel(*refs):
    refs = list(refs)
    take = lambda n: [refs.pop(0) for _ in range(n)]
    weights = dict(zip(MATS, take(5)))
    small_own, block_in = take(2)
    outputs = dict(zip(MATS, take(5)))
    small_low, ns_out, nst_out, middle_out, gates_out, taps_out, nft_out, got_out = take(8)
    own = dict(zip(MATS, take(5)))
    in_full, out_full, small_full = take(3)
    ns, nst, middle, gates, taps, nft, got, normed, gate_c, ext, halo_out, halo_in = take(12)
    local_sem, send_sem, recv_sem = take(3)
    full = dict(outputs, **{"in": in_full, "out": out_full})
    me = coords()
    links = Links(me, send_sem, recv_sem)
    units = [(name, t) for name in MATS for t in range(THIRDS[name])]

    copies = []

    def copy(src, dst):
        cp = pltpu.make_async_copy(src, dst, local_sem.at[len(copies)])
        cp.start()
        copies.append(cp)

    for name in MATS:
        for spot, rows, cols in own_spots(name):
            own[name][spot] = weights[name][rows, cols].astype(jnp.bfloat16)
    small_full[me["z"], me["x"], me["c"]] = small_own[...]
    for name, t in units:
        q = ALL if t == 0 else me["y"]
        piece = third(name, t)
        copy(own_view(own[name], name, piece, q), view(full[name], name, piece, dict(me, y=q)))
    meet(me)
    for cp in copies:
        cp.wait()
    placed = len(copies)

    def send(u, at, axis, by, half=None):
        piece = view(full[u[0]], u[0], third(*u), at, half)
        return links.send(lambda: (piece, piece), axis, by)

    at_of = {u: dict(me, y=ALL) if u[1] == 0 else dict(me) for u in units}
    pending = {}
    swaps = {u: [] for u in units}

    def advance(u, step):
        order = GATHER_ORDER[u[1]]
        skipped = 3 - len(order)
        if step < 2 * skipped:
            return
        if step > 2 * skipped and step % 2 == 0:
            for cp in pending[u]:
                cp.wait_recv()
            done = order[step // 2 - 1 - skipped]
            if step == 6:
                swaps[u].append(send(u, shifted(at_of[u], done, 2), "c", 1))
                return
            at_of[u] = dict(at_of[u], **{done: ALL})
        axis = order[step // 2 - skipped]
        at = at_of[u]
        if step % 2 == 0:
            pending[u] = [send(u, at, axis, 1), send(u, at, axis, 3)]
            if step == 4:
                swaps[u].append(send(u, at, "c", 1))
            return
        sends = []
        for side, by in enumerate((1, 3)):
            pending[u][side].wait_recv()
            came = shifted(at, axis, 4 - by)
            sends.append(send(u, came, axis, by, side))
            if step == 5:
                swaps[u].append(send(u, came, "c", 1))
        pending[u] = sends

    groups = {"A": [u for u in units if u[0] in ("in", "out")]}
    groups.update({k: [u for u in units if u[0] == n] for k, n in (("G", "gate"), ("U", "up"), ("D", "down"))})

    def run(plan):
        for item in zip(plan[::2], plan[1::2]):
            for u in groups[item[0]]:
                advance(u, int(item[1]))

    small_at = [dict(me)]
    small_cps = []

    def small_step(axis):
        for cp in small_cps:
            cp.wait_recv()
        if small_cps:
            small_at[0] = dict(small_at[0], **{"z" if axis == "x" else "x": ALL})
        at = small_at[0]
        piece = small_full.at[at["z"], at["x"], at["c"]]
        steps = (1,) if axis == "c" else (1, 2, 3)
        small_cps[:] = [links.send(lambda: (piece, piece), axis, s) for s in steps]

    small_step("z")
    run("A0G0U0D0A1G1U1D1")
    small_step("x")
    run("A2G2U2D2A3G3U3D3")
    small_step("c")
    run("A4G4A5U4D4")

    for cp in small_cps:
        cp.wait_recv()
    for k in range(8):
        z, x = k // 2, 2 * (k % 2)
        small_low[:, 128 * k : 128 * k + 128] = (
            small_full[z, x, 0] + small_full[z, x, 1] + small_full[z, x + 1, 0] + small_full[z, x + 1, 1]
        )
    tokens = block_in[...].astype(jnp.float32)
    low = (tokens * norm_scale(tokens) * small_low[3:4]).astype(jnp.bfloat16)
    normed[...] = low
    nft[...] = low.T
    copy(nft, nft_out)
    run("A6")
    for u in groups["A"]:
        for cp in swaps[u]:
            cp.wait_recv()

    def conv_work():
        for q in range(4):
            cols = slice(256 * q, 256 * q + 256)
            cuts = []
            for t in range(3):
                weight = in_full[t, q].reshape(1024, 256)
                cuts.append(dot_nn(normed[...], weight))
            gate_c[:, cols] = cuts[1]
            for t in range(3):
                gates[t, :, cols] = cuts[t].astype(jnp.bfloat16)
            mixed = (cuts[0] * cuts[2]).astype(jnp.bfloat16)
            for m in range(MICRO):
                halo_out[m, :, cols] = mixed[128 * m + 112 : 128 * m + 128]
                ext[m, 8:136, cols] = mixed[128 * m : 128 * m + 128].astype(jnp.float32)
            yield
        sent = links.send_to(lambda: (halo_out, halo_in), lambda: along(me, 1))
        copy(in_full, outputs["in"])
        copy(out_full, outputs["out"])
        yield
        sent.wait_recv()
        keep = (me["z"] * 8 + me["x"] * 2 + me["c"] != 0).astype(jnp.float32)
        for m in range(MICRO):
            ext[m, 0:8] = halo_in[m].astype(jnp.float32)[8:16] * keep
        for m in range(MICRO):
            rows = slice(128 * m, 128 * m + 128)
            conv = small_low[0:1] * ext[m, 8:136]
            for k in range(1, KW):
                conv += small_low[k : k + 1] * ext[m, 8 - k : 136 - k]
            for k in range(KW):
                taps[k, rows] = ext[m, 8 - k : 136 - k].astype(jnp.bfloat16)
            gates[3, rows] = conv.astype(jnp.bfloat16)
            normed[rows] = (gate_c[rows] * conv).astype(jnp.bfloat16)
            yield
        copy(gates, gates_out)
        copy(taps, taps_out)
        got[...] = normed[...].T
        copy(got, got_out)
        yield
        for q in range(4):
            cols = slice(256 * q, 256 * q + 256)
            weight = out_full[q].reshape(1024, 256)
            middle[:, cols] = block_in[:, cols].astype(jnp.float32) + dot_nn(normed[...], weight)
        copy(middle, middle_out)
        yield
        field = middle[...]
        ns[...] = (field * norm_scale(field) * small_low[4:5]).astype(jnp.bfloat16)
        copy(ns, ns_out)
        nst[...] = ns[...].T
        copy(nst, nst_out)
        yield

    work = conv_work()
    for step in (5, 6):
        for key in "GUD":
            for u in groups[key]:
                next(work, None)
                advance(u, step)
    for _ in work:
        pass
    for key in "GUD":
        for u in groups[key]:
            for cp in swaps[u]:
                cp.wait_recv()
    for cp in copies[placed:]:
        cp.wait()
    links.finish()


def forward(weights, small, block_in):
    small_rows = jnp.pad(small.astype(jnp.bfloat16).astype(jnp.float32), ((0, 3), (0, 0)))
    lane = lax.broadcasted_iota(jnp.int32, (8, 128), 1) // 32
    small_own = jnp.where(lane == lax.axis_index("fsdp") % 4, jnp.tile(small_rows, (1, 4)), 0.0)
    in_vmem = pl.BlockSpec(memory_space=pltpu.VMEM)
    anywhere = pl.BlockSpec(memory_space=pl.ANY)
    bf16, f32 = jnp.bfloat16, jnp.float32
    kept = [
        ((256, 1024), bf16),
        ((1024, 256), bf16),
        ((256, 1024), f32),
        ((4, 256, 1024), bf16),
        ((3, 256, 1024), bf16),
        ((1024, 256), bf16),
        ((1024, 256), bf16),
    ]
    outs = pl.pallas_call(
        forward_kernel,
        out_shape=[jax.ShapeDtypeStruct(FULL[name], bf16) for name in MATS]
        + [jax.ShapeDtypeStruct((8, 1024), f32)]
        + [jax.ShapeDtypeStruct(*k) for k in kept],
        in_specs=[in_vmem] * 7,
        out_specs=[anywhere] * 5 + [in_vmem] + [anywhere] * 7,
        scratch_shapes=[pltpu.VMEM(OWN[name], bf16) for name in MATS]
        + [pltpu.VMEM(FULL["in"], bf16), pltpu.VMEM(FULL["out"], bf16)]
        + [pltpu.VMEM((4, 4, 2, 8, 128), f32)]
        + [pltpu.VMEM(*k) for k in kept]
        + [
            pltpu.VMEM((256, 1024), bf16),
            pltpu.VMEM((256, 1024), f32),
            pltpu.VMEM((2, 136, 1024), f32),
            pltpu.VMEM((2, 16, 1024), bf16),
            pltpu.VMEM((2, 16, 1024), bf16),
            pltpu.SemaphoreType.DMA((32,)),
            pltpu.SemaphoreType.DMA((256,)),
            pltpu.SemaphoreType.DMA((256,)),
        ],
        compiler_params=pltpu.CompilerParams(
            collective_id=1, has_side_effects=True, vmem_limit_bytes=VMEM_BYTES
        ),
        name="forward",
    )(*weights, small_own, block_in)
    return outs[0:5], outs[5:]


def norm_back(grad_normed, field, gain):
    scale = norm_scale(field)
    normed = field * scale
    weighted = grad_normed * gain
    grad_field = scale * (weighted - normed * jnp.mean(weighted * normed, axis=-1, keepdims=True))
    return (grad_field, jnp.sum(grad_normed * normed, axis=0, keepdims=True))


def order_of(name, t):
    if name == "gate":
        return SUM_ORDER[(2 * t) % 3]
    if name == "up":
        return SUM_ORDER[(2 * t + 1) % 3]
    return SUM_ORDER[t]


BATCHES = [[("gate", j), ("up", j)] for j in range(FF_BLOCKS)]
BATCHES += [[("down", t) for t in range(3)], [("out", 0), ("out", 1)], [("in", t) for t in range(3)]]
UNITS = [u for batch in BATCHES for u in batch]


def tiles(name):
    return BLOCK[name][0] // 16, BLOCK[name][1] // 128


def tile_count(name):
    return tiles(name)[0] * tiles(name)[1]


def landing(unit):
    k = tile_count(unit[0])
    return [
        ((2, 2, 4, k, 16, 128), (2, 4, 4, k, 16, 128)),
        ((2, 2, k, 16, 128), (2, 4, k, 16, 128)),
        ((2, k // 2, 16, 128), (2, k, 16, 128)),
    ]


def part(ref, unit, at, half=None):
    name, t = unit
    index = [at[a] for a in order_of(*unit)] + [ALL]
    if half is not None:
        size = (4, 4, 4, tile_count(name))
        i = next(i for i in range(4) if index[i] is ALL)
        index[i] = pl.ds(half * (size[i] // 2), size[i] // 2)
    return ref.at[(t,) + tuple(index)]


def run_of(ref, unit, first):
    return ref.at[pl.ds(first, 64 * tile_count(unit[0]))]


LAG = 1
EVERY = {"y": ALL, "z": ALL, "x": ALL}


class Sums:
    def __init__(self, me, links, mine, theirs, outs, staging, slots, slot_sem, land):
        self.me, self.links = me, links
        self.mine, self.theirs, self.outs = mine, theirs, outs
        self.staging, self.slots, self.slot_sem, self.land = staging, slots, slot_sem, land
        self.at = {u: dict(EVERY) for u in UNITS}
        self.swaps, self.loads, self.pending, self.last = {}, {}, {}, []
        self.users = []

    def first(self, unit, slots):
        k = UNITS.index(unit)
        return 128 * (k % slots) if k < 2 * FF_BLOCKS else 384 * (k % (slots // 2))

    def room(self, unit):
        first, count = self.first(unit, 4), 64 * tile_count(unit[0])
        for low, high, user in self.users:
            if low < first + count and first < high and id(user) not in self.links.done:
                self.links.left(user)
        return first

    def swap(self, unit):
        first, count = self.first(unit, 4), 64 * tile_count(unit[0])

        def ends():
            place = run_of(self.theirs[unit[0]], unit, count * unit[1])
            return run_of(self.staging, unit, first), place

        self.swaps[unit] = self.links.send(ends, "c", 1)
        self.users.append((first, first + count, self.swaps[unit]))

    def load(self, unit):
        self.swaps[unit].wait_recv()
        src = run_of(self.theirs[unit[0]], unit, 64 * tile_count(unit[0]) * unit[1])
        dst = run_of(self.slots, unit, self.first(unit, 2))
        cp = pltpu.make_async_copy(src, dst, self.slot_sem.at[UNITS.index(unit)])
        cp.start()
        self.loads[unit] = cp

    def join(self, unit):
        self.loads[unit].wait()
        total = part(self.mine[unit[0]], unit, EVERY)
        first, k = self.first(unit, 2), tile_count(unit[0])

        def step(i, carry):
            spot = (i // 4, i % 4)
            fresh = self.slots[pl.ds(first + 4 * k * i, 4 * k)].reshape(4, k, 16, 128)
            total[spot] = total[spot] + fresh
            return carry

        lax.fori_loop(0, 16, step, 0, unroll=2)
        self.start(unit, 0)

    def add(self, unit, p, at, half, *landed):
        ref = part(self.mine[unit[0]], unit, at, half)
        if p > 0:
            self.add_block(ref, ALL, *landed)
            return

        def step(i, carry):
            self.add_block(ref, i, *landed)
            return carry

        lax.fori_loop(0, 4 if half is None else 2, step, 0, unroll=2)

    def add_block(self, ref, i, *landed):
        if len(landed) == 1:
            ref[i] = ref[i] + landed[0][i]
            return
        total = ref[i].astype(jnp.float32)
        for value in landed:
            total = total + value[i].astype(jnp.float32)
        ref[i] = total.astype(jnp.bfloat16)

    def spot(self, at, axis, by):
        return dict(at, **{axis: (self.me[axis] + by) % 4})

    def start(self, unit, p):
        axis = order_of(*unit)[p]
        at = self.at[unit]
        halves = self.land[unit][p][0]
        ref = self.mine[unit[0]]

        def ends(side):
            return lambda: (part(ref, unit, self.spot(at, axis, 2), side), halves.at[side])

        self.pending[unit] = [
            self.links.send(ends(0), axis, 1),
            self.links.send(ends(1), axis, 3),
        ]

    def middle(self, unit, p):
        axis = order_of(*unit)[p]
        at = self.at[unit]
        halves, blocks = self.land[unit][p]
        ref = self.mine[unit[0]]
        sends = []

        def ends(side, by):
            return lambda: (part(ref, unit, self.spot(at, axis, by)), blocks.at[side])

        for side, by in enumerate((1, 3)):
            self.pending[unit][side].wait_recv()
            self.add(unit, p, self.spot(at, axis, by), side, halves.at[side])
            sends.append(self.links.send(ends(side, by), axis, by))
        self.pending[unit] = sends

    def end(self, unit, p):
        axis = order_of(*unit)[p]
        blocks = self.land[unit][p][1]
        for cp in self.pending[unit]:
            cp.wait_recv()
        self.at[unit] = dict(self.at[unit], **{axis: self.me[axis]})
        self.add(unit, p, self.at[unit], None, blocks.at[0], blocks.at[1])
        if p < 2:
            self.start(unit, p + 1)
            return

        def mine_out():
            return self.outs[unit[0]].at[unit[1], self.me["y"]]

        mine_out()[...] = part(self.mine[unit[0]], unit, self.at[unit])[...]
        for by in (1, 2, 3):
            self.last.append(self.links.send(lambda: (mine_out(), mine_out()), "y", by))

    def stage(self, s, batch):
        for unit in batch:
            if s % 2 == 0:
                self.middle(unit, s // 2)
            else:
                self.end(unit, s // 2)


def backward_kernel(*refs):
    refs = list(refs)
    take = lambda n: [refs.pop(0) for _ in range(n)]
    ns, g, small_low = take(3)
    nst_hbm, wg, wu, wd, w_in, w_out = take(6)
    middle_hbm, tokens_hbm, gates_hbm, taps_hbm, nft_hbm, got_hbm = take(6)
    outs = dict(zip(MATS, take(5)))
    small_out, block_out, input_grad = take(3)
    theirs = dict(zip(MATS, take(5)))
    mine = dict(zip(MATS, take(5)))
    land = {u: [tuple(take(2)) for _ in range(3)] for u in UNITS}
    staging, slots, hidden_t, grad_ns, ff_out, nst = take(6)
    halo_out, halo_in, small_land = take(3)
    local_sem, slot_sem, send_sem, recv_sem = take(4)
    me = coords()
    links = Links(me, send_sem, recv_sem)
    sums = Sums(me, links, mine, theirs, outs, staging, slots, slot_sem, land)

    def first_loads(wg_s, wu_s, wd_s):
        def fetch(j):
            s = j % 2
            pairs = [
                (wg.at[j], wg_s.at[s]),
                (wu.at[j], wu_s.at[s]),
                (wd.at[:, pl.ds(512 * j, 512)], wd_s.at[s]),
            ]
            cps = [
                pltpu.make_async_copy(a, b, local_sem.at[3 * s + i]) for i, (a, b) in enumerate(pairs)
            ]
            for cp in cps:
                cp.start()
            return cps

        return fetch

    def drive(tick, work):
        tasks = []
        if 0 <= tick - 1 < len(BATCHES):
            batch = BATCHES[tick - 1]
            ahead = 2 if tick - 1 < FF_BLOCKS else 1
            for unit in batch[:ahead]:
                sums.load(unit)

            def joins():
                for i, unit in enumerate(batch):
                    if i >= ahead:
                        sums.load(unit)
                    sums.join(unit)

            tasks.append(joins)
        for s in range(6):
            if 0 <= tick - 1 - LAG * (s + 1) < len(BATCHES):
                tasks.append(functools.partial(sums.stage, s, BATCHES[tick - 1 - LAG * (s + 1)]))
        for _ in work if work is not None else ():
            for _ in range(2):
                if tasks:
                    tasks.pop(0)()
        for task in tasks:
            task()

    def spread(name, t, value, half):
        unit = (name, t)
        rows, cols = BLOCK[name]
        down, across = tiles(name)
        first = sums.room(unit) if half == 1 else None
        for q in range(4):
            for h in range(across):
                for z in range(4):
                    piece = value[4 * rows * z : 4 * rows * (z + 1), cols * q + 128 * h :][:, 0:128]
                    piece = piece.astype(jnp.bfloat16).reshape(4, down, 16, 128)
                    kinds = slice(down * h, down * h + down)
                    if half == 0:
                        at = {"z": z, "y": q, "x": ALL}
                        spot = tuple(at[a] for a in order_of(*unit))
                        mine[name][(t,) + spot + (kinds,)] = piece
                        continue
                    for x in range(4):
                        at = {"z": z, "y": q, "x": x}
                        i, j, k = (at[a] for a in order_of(*unit))
                        start = first + (16 * i + 4 * j + k) * down * across + down * h
                        staging[start : start + down] = piece[x]
        if half == 1:
            sums.swap((name, t))

    def ff_block(j, wg_s, wu_s, wd_s, fetch, fetched):
        for cp in fetched[j]:
            cp.wait()
        if j + 1 < FF_BLOCKS:
            fetched[j + 1] = fetch(j + 1)
        s = j % 2
        gate_w = jnp.concatenate([wg_s[s, q] for q in range(4)], axis=1)
        up_w = jnp.concatenate([wu_s[s, q] for q in range(4)], axis=1)
        gate_pre = dot_nn(ns[...], gate_w)
        up_pre = dot_nn(ns[...], up_w)
        grad_hidden = dot_nt(g[:, 0:256], wd_s[s, 0])
        for q in range(1, 4):
            grad_hidden += dot_nt(g[:, 256 * q : 256 * q + 256], wd_s[s, q])
        sig = jax.nn.sigmoid(gate_pre)
        silu = gate_pre * sig
        hidden = (silu * up_pre).astype(jnp.bfloat16)
        grad_gate = (grad_hidden * up_pre * sig * (1.0 + gate_pre * (1.0 - sig))).astype(
            jnp.bfloat16
        )
        grad_up = (grad_hidden * silu).astype(jnp.bfloat16)
        for half in (1, 0):
            spread("gate", j, dot_nn(nst[half].reshape(512, 256), grad_gate), half)
            spread("up", j, dot_nn(nst[half].reshape(512, 256), grad_up), half)
        yield
        turned = hidden.T
        for k in range(32):
            row = 512 * j + 16 * k
            f, r = row // 144, row % 144
            hidden_t[f // 2, f % 2, r : r + 16, :] = turned[16 * k : 16 * k + 16]
        fresh = dot_nt(grad_gate, gate_w) + dot_nt(grad_up, up_w)
        if j == 0:
            grad_ns[...] = fresh
        else:
            grad_ns[...] += fresh
        for q in range(4):
            cols = slice(256 * q, 256 * q + 256)
            if j == 0:
                ff_out[:, cols] = dot_nn(hidden, wd_s[s, q])
            else:
                ff_out[:, cols] += dot_nn(hidden, wd_s[s, q])
        yield

    def feed_forward(wg_s, wu_s, wd_s):
        fetch = first_loads(wg_s, wu_s, wd_s)
        by_core = [
            pltpu.make_async_copy(nst_hbm.at[:, (me["c"] + h) % 2], nst.at[h], local_sem.at[6 + h])
            for h in (0, 1)
        ]
        for cp in by_core:
            cp.start()
        fetched = {0: fetch(0)}
        meet(me)
        for cp in by_core:
            cp.wait()
        for j in range(FF_BLOCKS):
            drive(j, ff_block(j, wg_s, wu_s, wd_s, fetch, fetched))

    pl.run_scoped(
        feed_forward,
        pltpu.VMEM((2, 4, 1024, 128), jnp.bfloat16),
        pltpu.VMEM((2, 4, 1024, 128), jnp.bfloat16),
        pltpu.VMEM((2, 4, 512, 256), jnp.bfloat16),
    )

    def give_input_grad():
        return pltpu.make_async_copy(ff_out, input_grad, local_sem.at[15])

    small_at = [0]
    small_cps = []

    def small_send(axis):
        steps = (1,) if axis == "c" else (1, 2, 3)
        first = small_at[0]
        small_at[0] += len(steps)
        small_cps[:] = [
            links.send(lambda s=s: (small_out, small_land.at[first + s - 1]), axis, s)
            for s in steps
        ]

    def small_take():
        first = small_at[0] - len(small_cps)
        for cp in small_cps:
            cp.wait_recv()
        for cp in small_cps:
            links.left(cp)
        total = small_out[...]
        for s in range(len(small_cps)):
            total = total + small_land[first + s]
        small_out[...] = total

    def conv_branch(middle, tokens, gates, taps_in, nft, got, wi_s, conv_ext, grad_proj):
        wo_s, grad_in = wi_s.at[1], ff_out
        sources = [middle_hbm, tokens_hbm, gates_hbm, taps_hbm, w_out]
        places = [middle, tokens, gates, taps_in, wo_s]
        for h in (0, 1):
            sources += [nft_hbm.at[:, (me["c"] + h) % 2], got_hbm.at[:, (me["c"] + h) % 2]]
            places += [nft.at[h], got.at[h]]
        cps = [pltpu.make_async_copy(a, b, local_sem.at[i]) for i, (a, b) in enumerate(zip(sources, places))]
        for cp in cps:
            cp.start()
        fetched = {}

        def fetch(t):
            fetched[t] = pltpu.make_async_copy(
                w_in.at[pl.ds(4 * t, 4)], wi_s.at[t % 2], local_sem.at[10 + t]
            )
            fetched[t].start()

        fetch(0)

        def down_work():
            for t in range(3):
                for half in (1, 0):
                    c = (me["c"] + half) % 2
                    left = hidden_t[:, c, 48 * t : 48 * t + 48, :].reshape(768, 256)
                    spread("down", t, dot_nn(left, g[...]), half)
                yield

        drive(9, down_work())
        for cp in cps:
            cp.wait()

        def out_work():
            gain_second = small_low[4:5]
            block_out[...] = (middle[...] + ff_out[...]).astype(jnp.bfloat16)
            grad_norm, grad_gain = norm_back(grad_ns[...], middle[...], gain_second)
            small_out[4:5] = grad_gain
            grad_middle = g[...].astype(jnp.float32) + grad_norm
            middle[...] = grad_middle
            grad_branch = grad_middle.astype(jnp.bfloat16)
            for half in (1, 0):
                whole = dot_nn(got[half].reshape(512, 256), grad_branch).reshape(16, 2, 16, 1024)
                for t in range(2):
                    spread("out", t, whole[:, t].reshape(256, 1024), half)
            yield
            grad_gated = dot_nt(grad_branch[:, 0:256], wo_s[0])
            for q in range(1, 4):
                grad_gated += dot_nt(grad_branch[:, 256 * q : 256 * q + 256], wo_s[q])
            grad_conv = (grad_gated * gates[1].astype(jnp.float32)).astype(jnp.bfloat16)
            for m in range(MICRO):
                halo_out[m] = grad_conv[128 * m : 128 * m + 16]
            sent = links.send_to(lambda: (halo_out, halo_in), lambda: along(me, 31))
            grad_proj[:, 1024:2048] = (grad_gated * gates[3].astype(jnp.float32)).astype(jnp.bfloat16)
            wide = grad_conv.astype(jnp.float32)
            for m in range(MICRO):
                conv_ext[m, 0:128] = wide[128 * m : 128 * m + 128]
            for k in range(KW):
                small_out[k : k + 1] = jnp.sum(
                    wide * taps_in[k].astype(jnp.float32), axis=0, keepdims=True
                )
            yield
            sent.wait_recv()
            keep = (me["z"] * 8 + me["x"] * 2 + me["c"] != 31).astype(jnp.float32)
            for m in range(MICRO):
                conv_ext[m, 128:136] = halo_in[m].astype(jnp.float32)[0:8] * keep
            for m in range(MICRO):
                mixed = small_low[0:1] * conv_ext[m, 0:128]
                for k in range(1, KW):
                    mixed += small_low[k : k + 1] * conv_ext[m, k : k + 128]
                rows = slice(128 * m, 128 * m + 128)
                grad_proj[rows, 0:1024] = (mixed * gates[2, rows].astype(jnp.float32)).astype(
                    jnp.bfloat16
                )
                grad_proj[rows, 2048:3072] = (mixed * gates[0, rows].astype(jnp.float32)).astype(
                    jnp.bfloat16
                )

        drive(10, out_work())
        fetch(1)

        def in_work():
            for t in range(3):
                cols = slice(1024 * t, 1024 * t + 1024)
                for half in (1, 0):
                    spread("in", t, dot_nn(nft[half].reshape(512, 256), grad_proj[:, cols]), half)
                yield

        drive(11, in_work())

        def token_work():
            for t in range(3):
                fetched[t].wait()
                for q in range(4):
                    cols = slice(256 * (4 * t + q), 256 * (4 * t + q) + 256)
                    fresh = dot_nt(grad_proj[:, cols], wi_s[t % 2, q])
                    if t == 0 and q == 0:
                        grad_in[...] = fresh
                    else:
                        grad_in[...] += fresh
                if t == 0:
                    fetch(2)
                yield
            x = tokens[...].astype(jnp.float32)
            grad_norm, grad_gain = norm_back(grad_in[...], x, small_low[3:4])
            small_out[3:4] = grad_gain
            small_out[5:8] = jnp.zeros((3, 1024), jnp.float32)
            grad_in[...] = middle[...] + grad_norm
            give_input_grad().start()
            small_send("c")

        drive(12, token_work())

    pl.run_scoped(
        conv_branch,
        pltpu.VMEM((256, 1024), jnp.float32),
        pltpu.VMEM((256, 1024), jnp.bfloat16),
        pltpu.VMEM((4, 256, 1024), jnp.bfloat16),
        pltpu.VMEM((3, 256, 1024), jnp.bfloat16),
        pltpu.VMEM((2, 16, 32, 256), jnp.bfloat16),
        pltpu.VMEM((2, 16, 32, 256), jnp.bfloat16),
        pltpu.VMEM((2, 4, 1024, 256), jnp.bfloat16),
        pltpu.VMEM((2, 136, 1024), jnp.float32),
        pltpu.VMEM((256, 3072), jnp.bfloat16),
    )
    for i, axis in enumerate("xzy"):
        drive(13 + i, None)
        small_take()
        small_send(axis)
    drive(16, None)
    small_take()
    for tick in range(17, len(BATCHES) + 1 + 6 * LAG):
        drive(tick, None)
    for cp in sums.last:
        cp.wait_recv()
    give_input_grad().wait()
    links.finish()


def backward(ns, g, small_low, nst, w_gate, w_up, w_down, w_in, w_out, middle, tokens, *rest):
    in_vmem = pl.BlockSpec(memory_space=pltpu.VMEM)
    anywhere = pl.BlockSpec(memory_space=pl.ANY)
    tiled = {}
    for name in MATS:
        pieces = FULL[name][0 if name in BY_THIRD else 4]
        tiled[name] = (pieces, tile_count(name))
    scratch = [pltpu.VMEM((n, 4, 4, 4, k, 16, 128), jnp.bfloat16) for n, k in tiled.values()]
    for u in UNITS:
        for halves, blocks in landing(u):
            scratch += [pltpu.VMEM(halves, jnp.bfloat16), pltpu.VMEM(blocks, jnp.bfloat16)]
    scratch += [
        pltpu.VMEM((768, 16, 128), jnp.bfloat16),
        pltpu.VMEM((384, 16, 128), jnp.bfloat16),
        pltpu.VMEM((16, 2, 144, 256), jnp.bfloat16),
        pltpu.VMEM((256, 1024), jnp.float32),
        pltpu.VMEM((256, 1024), jnp.float32),
        pltpu.VMEM((2, 16, 32, 256), jnp.bfloat16),
        pltpu.VMEM((2, 16, 1024), jnp.bfloat16),
        pltpu.VMEM((2, 16, 1024), jnp.bfloat16),
        pltpu.VMEM((10, 8, 1024), jnp.float32),
        pltpu.SemaphoreType.DMA((16,)),
        pltpu.SemaphoreType.DMA((len(UNITS),)),
        pltpu.SemaphoreType.DMA((480,)),
        pltpu.SemaphoreType.DMA((480,)),
    ]
    outs = pl.pallas_call(
        backward_kernel,
        out_shape=[jax.ShapeDtypeStruct((n, 4, k, 16, 128), jnp.bfloat16) for n, k in tiled.values()]
        + [
            jax.ShapeDtypeStruct((8, 1024), jnp.float32),
            jax.ShapeDtypeStruct((256, 1024), jnp.bfloat16),
            jax.ShapeDtypeStruct((256, 1024), jnp.float32),
        ]
        + [jax.ShapeDtypeStruct((n * 64 * k, 16, 128), jnp.bfloat16) for n, k in tiled.values()],
        in_specs=[in_vmem] * 3 + [anywhere] * 12,
        out_specs=[in_vmem] * 7 + [anywhere] * 6,
        scratch_shapes=scratch,
        compiler_params=pltpu.CompilerParams(
            collective_id=2, has_side_effects=True, vmem_limit_bytes=VMEM_BYTES
        ),
        name="backward",
    )(ns, g, small_low, nst, w_gate, w_up, w_down, w_in, w_out, middle, tokens, *rest)
    return outs[0:5], outs[5], outs[6], outs[7]


def adam_update(weight, first, second, gradient, step_rate, decay_rate):
    first_new = beta_one * first + (1.0 - beta_one) * gradient
    second_new = beta_two * second + (1.0 - beta_two) * gradient * gradient
    corrected = (
        first_new
        / (1.0 - beta_one**STEP)
        / (jnp.sqrt(second_new / (1.0 - beta_two**STEP)) + adam_eps)
    )
    return (weight - step_rate * (corrected + decay_rate * weight), first_new, second_new)


def adam_kernel(*refs):
    sources = [dict(zip(MATS, refs[5 * i : 5 * i + 5])) for i in range(4)]
    results = [dict(zip(MATS, refs[20 + 5 * i : 25 + 5 * i])) for i in range(3)]
    weights, firsts, seconds, sums = sources

    def update(name):
        rows, cols = BLOCK[name]
        down, across = tiles(name)
        for t in range(sums[name].shape[0]):
            for q in range(4):
                for h in range(across):
                    if name in BY_THIRD:
                        top, left = 0, (4 * t + q) * cols + 128 * h
                    else:
                        top, left = t * rows, q * cols + 128 * h
                    spot = (slice(top, top + rows), slice(left, left + 128))
                    gradient = sums[name][t, q, down * h : down * h + down].reshape(rows, 128)
                    new = adam_update(
                        weights[name][spot],
                        firsts[name][spot],
                        seconds[name][spot],
                        gradient.astype(jnp.float32),
                        rate_matrix,
                        weight_decay,
                    )
                    for result, value in zip(results, new):
                        result[name][spot] = value

    for name in ("in", "gate", "up", "down"):
        update(name)

    @pl.when(pl.program_id(0) == 0)
    def _():
        update("out")


def adam(weights, firsts, seconds, sums):
    shard = {
        "in": pl.BlockSpec((32, 1024), lambda i: (0, i)),
        "out": pl.BlockSpec((32, 1024), lambda i: (0, 0)),
        "gate": pl.BlockSpec((32, 1536), lambda i: (0, i)),
        "up": pl.BlockSpec((32, 1536), lambda i: (0, i)),
        "down": pl.BlockSpec((48, 1024), lambda i: (i, 0)),
    }
    pieces = {
        "in": pl.BlockSpec((1, 4, 4, 16, 128), lambda i: (i, 0, 0, 0, 0)),
        "out": pl.BlockSpec((2, 4, 2, 16, 128), lambda i: (0, 0, 0, 0, 0)),
        "gate": pl.BlockSpec((3, 4, 2, 16, 128), lambda i: (i, 0, 0, 0, 0)),
        "up": pl.BlockSpec((3, 4, 2, 16, 128), lambda i: (i, 0, 0, 0, 0)),
        "down": pl.BlockSpec((1, 4, 6, 16, 128), lambda i: (i, 0, 0, 0, 0)),
    }
    in_order = [shard[name] for name in MATS]
    outs = pl.pallas_call(
        adam_kernel,
        grid=(3,),
        in_specs=in_order * 3 + [pieces[name] for name in MATS],
        out_specs=in_order * 3,
        out_shape=[jax.ShapeDtypeStruct(w.shape, jnp.float32) for w in weights] * 3,
        compiler_params=pltpu.CompilerParams(vmem_limit_bytes=VMEM_BYTES),
        name="adam",
    )(*weights, *firsts, *seconds, *sums)
    return outs[0:5], outs[5:10], outs[10:15]


def body(
    block_input,
    cotangent,
    in_weight,
    out_weight,
    gate_weight,
    up_weight,
    down_weight,
    small_params,
    in_first,
    out_first,
    gate_first,
    up_first,
    down_first,
    small_first,
    in_second,
    out_second,
    gate_second,
    up_second,
    down_second,
    small_second,
):
    rows = block_input.shape[1]
    tokens = block_input.reshape(256, 1024)
    full, kept = forward(
        (in_weight, out_weight, gate_weight, up_weight, down_weight), small_params, tokens
    )
    small_low, ns, nst, middle, gates, taps, nft, got = kept
    cuts = (16, 2, 32, 256)
    summed, small_sum, block_out, input_grad = backward(
        ns,
        cotangent.reshape(256, 1024),
        small_low,
        nst.reshape(cuts),
        full[2].reshape(9, 4, 1024, 128),
        full[3].reshape(9, 4, 1024, 128),
        full[4].reshape(4, 4608, 256),
        full[0].reshape(12, 1024, 256),
        full[1].reshape(4, 1024, 256),
        middle,
        tokens,
        gates,
        taps,
        nft.reshape(cuts),
        got.reshape(cuts),
    )
    position = lax.axis_index("fsdp")
    small_mine = lax.dynamic_slice(small_sum, (0, position * 32), (5, 32))
    new_weights, new_firsts, new_seconds = adam(
        (in_weight, out_weight, gate_weight, up_weight, down_weight),
        (in_first, out_first, gate_first, up_first, down_first),
        (in_second, out_second, gate_second, up_second, down_second),
        summed,
    )
    new_small = adam_update(small_params, small_first, small_second, small_mine, rate_small, 0.0)
    return (
        block_out.reshape(MICRO, rows, 1024),
        input_grad.reshape(MICRO, rows, 1024),
        *new_weights,
        new_small[0],
        *new_firsts,
        new_small[1],
        *new_seconds,
        new_small[2],
    )


def solution(mesh):
    acts = P(None, ("dp", "fsdp"), None)
    params = (P("fsdp", None),) * 5 + (P(None, "fsdp"),)
    return jax.shard_map(
        body,
        mesh=mesh,
        in_specs=(acts, acts) + params * 3,
        out_specs=(acts, acts) + params * 3,
        check_vma=False,
    )
```

```python
import functools

import jax
import jax.numpy as jnp
from jax import lax
from jax.experimental import pallas as pl
from jax.experimental.pallas import tpu as pltpu
from jax.sharding import PartitionSpec as P

MESH = pl.DeviceIdType.MESH
KW = 3
MICRO = 2
STEP = 10

norm_eps = 1e-05
beta_one = 0.9
beta_two = 0.95
adam_eps = 1e-08
rate_matrix = 0.02
rate_small = 0.4
weight_decay = 0.1

MATS = ("in", "out", "gate", "up", "down")
THIRDS = {"in": 3, "out": 2, "gate": 3, "up": 3, "down": 3}
FULL = {
    "in": (3, 4, 4, 4, 2, 32, 256),
    "out": (4, 4, 4, 2, 2, 16, 256),
    "gate": (9, 4, 4, 4, 2, 32, 128),
    "up": (9, 4, 4, 4, 2, 32, 128),
    "down": (4, 4, 4, 2, 3, 48, 256),
}
OWN = {
    "in": (3, 4, 32, 256),
    "out": (4, 2, 16, 256),
    "gate": (9, 4, 32, 128),
    "up": (9, 4, 32, 128),
    "down": (4, 3, 48, 256),
}
BLOCK = {"in": (32, 256), "out": (16, 256), "gate": (32, 128), "up": (32, 128), "down": (48, 256)}
BY_THIRD = ("in", "gate", "up")
GATHER_ORDER = {0: ("z", "x"), 1: ("x", "y", "z"), 2: ("z", "x", "y")}
SUM_ORDER = {0: ("x", "z", "y"), 1: ("z", "y", "x"), 2: ("y", "x", "z")}
ALL = slice(None)
VMEM_BYTES = 63 * 1024 * 1024
FF_BLOCKS = 9


def coords():
    y = lax.axis_index("dp")
    f = lax.axis_index("fsdp")
    return {"y": y, "z": f // 8, "x": (f // 2) % 4, "c": f % 2}


def device(at):
    return (at["y"], at["z"] * 8 + at["x"] * 2 + at["c"])


def shifted(at, axis, by):
    new = dict(at)
    new[axis] = (at[axis] + by) % (2 if axis == "c" else 4)
    return new


def along(me, by):
    f = (me["z"] * 8 + me["x"] * 2 + me["c"] + by) % 32
    return {"y": me["y"], "z": f // 8, "x": (f // 2) % 4, "c": f % 2}


def meet(me):
    sem = pltpu.get_barrier_semaphore()
    peers = [shifted(me, "c", 1)] + [shifted(me, a, s) for a in "xyz" for s in (1, 2, 3)]
    peers += [along(me, 1), along(me, 31)]
    for p in peers:
        pl.semaphore_signal(sem, inc=1, device_id=device(p), device_id_type=MESH)
    pl.semaphore_wait(sem, len(peers))


def half_of(name, half):
    if name in BY_THIRD:
        return (ALL if half is None else pl.ds(16 * half, 16), ALL)
    return (ALL, ALL if half is None else pl.ds(128 * half, 128))


def view(ref, name, t, at, half=None):
    tail = half_of(name, half)
    if name in BY_THIRD:
        return ref.at[(t, at["y"], at["z"], at["x"], at["c"]) + tail]
    return ref.at[(at["y"], at["z"], at["x"], at["c"], t) + tail]


def own_view(ref, name, t, q=ALL):
    if name in BY_THIRD:
        return ref.at[t, q]
    return ref.at[q, t]


class Copy:
    def __init__(self, links, index, ends, target):
        self.links, self.index, self.ends, self.target = links, index, ends, target

    def descriptor(self):
        src, dst = self.ends()
        return pltpu.make_async_remote_copy(
            src,
            dst,
            self.links.send_sem.at[self.index],
            self.links.recv_sem.at[self.index],
            device_id=device(self.target()),
            device_id_type=MESH,
        )

    def wait_recv(self):
        self.descriptor().wait_recv()

    def wait_send(self):
        self.descriptor().wait_send()


class Links:
    def __init__(self, me, send_sem, recv_sem):
        self.me, self.send_sem, self.recv_sem = me, send_sem, recv_sem
        self.sent = []
        self.done = set()

    def send(self, ends, axis, by):
        return self.send_to(ends, lambda: shifted(self.me, axis, by))

    def send_to(self, ends, target):
        cp = Copy(self, len(self.sent), ends, target)
        cp.descriptor().start()
        self.sent.append(cp)
        return cp

    def left(self, cp):
        cp.wait_send()
        self.done.add(id(cp))

    def finish(self):
        for cp in self.sent:
            if id(cp) not in self.done:
                cp.wait_send()


def dot_nt(left, right):
    return lax.dot_general(
        left, right, (((1,), (1,)), ((), ())), preferred_element_type=jnp.float32
    )


def dot_nn(left, right):
    return jnp.dot(left, right, preferred_element_type=jnp.float32)


def norm_scale(field):
    return lax.rsqrt(jnp.mean(field * field, axis=-1, keepdims=True) + norm_eps)


def third(name, t):
    return pl.ds(3 * t, 3) if name in ("gate", "up") else t


def own_spots(name):
    rows, cols = BLOCK[name]
    if name in BY_THIRD:
        return [
            ((t, q), slice(0, rows), slice((4 * t + q) * cols, (4 * t + q + 1) * cols))
            for t in range(OWN[name][0])
            for q in range(4)
        ]
    return [
        ((q, t), slice(t * rows, (t + 1) * rows), slice(q * cols, (q + 1) * cols))
        for q in range(4)
        for t in range(OWN[name][1])
    ]


def forward_kernel(*refs):
    refs = list(refs)
    take = lambda n: [refs.pop(0) for _ in range(n)]
    weights = dict(zip(MATS, take(5)))
    small_own, block_in = take(2)
    outputs = dict(zip(MATS, take(5)))
    small_low, ns_out, nst_out, middle_out, gates_out, taps_out, nft_out, got_out = take(8)
    own = dict(zip(MATS, take(5)))
    in_full, out_full, small_full = take(3)
    ns, nst, middle, gates, taps, nft, got, normed, gate_c, ext, halo_out, halo_in = take(12)
    local_sem, send_sem, recv_sem = take(3)
    full = dict(outputs, **{"in": in_full, "out": out_full})
    me = coords()
    links = Links(me, send_sem, recv_sem)
    units = [(name, t) for name in MATS for t in range(THIRDS[name])]

    copies = []

    def copy(src, dst):
        cp = pltpu.make_async_copy(src, dst, local_sem.at[len(copies)])
        cp.start()
        copies.append(cp)

    for name in MATS:
        for spot, rows, cols in own_spots(name):
            own[name][spot] = weights[name][rows, cols].astype(jnp.bfloat16)
    small_full[me["z"], me["x"], me["c"]] = small_own[...]
    for name, t in units:
        q = ALL if t == 0 else me["y"]
        piece = third(name, t)
        copy(own_view(own[name], name, piece, q), view(full[name], name, piece, dict(me, y=q)))
    meet(me)
    for cp in copies:
        cp.wait()
    placed = len(copies)

    def send(u, at, axis, by, half=None):
        piece = view(full[u[0]], u[0], third(*u), at, half)
        return links.send(lambda: (piece, piece), axis, by)

    at_of = {u: dict(me, y=ALL) if u[1] == 0 else dict(me) for u in units}
    pending = {}
    swaps = {u: [] for u in units}

    def advance(u, step):
        order = GATHER_ORDER[u[1]]
        skipped = 3 - len(order)
        if step < 2 * skipped:
            return
        if step > 2 * skipped and step % 2 == 0:
            for cp in pending[u]:
                cp.wait_recv()
            done = order[step // 2 - 1 - skipped]
            if step == 6:
                swaps[u].append(send(u, shifted(at_of[u], done, 2), "c", 1))
                return
            at_of[u] = dict(at_of[u], **{done: ALL})
        axis = order[step // 2 - skipped]
        at = at_of[u]
        if step < 4:
            if step % 2 == 0:
                pending[u] = [send(u, at, axis, by) for by in (1, 2, 3)]
            return
        if step % 2 == 0:
            pending[u] = [send(u, at, axis, 1), send(u, at, axis, 3)]
            if step == 4:
                swaps[u].append(send(u, at, "c", 1))
            return
        sends = []
        for side, by in enumerate((1, 3)):
            pending[u][side].wait_recv()
            came = shifted(at, axis, 4 - by)
            sends.append(send(u, came, axis, by, side))
            if step == 5:
                swaps[u].append(send(u, came, "c", 1))
        pending[u] = sends

    groups = {"A": [u for u in units if u[0] in ("in", "out")]}
    groups.update({k: [u for u in units if u[0] == n] for k, n in (("G", "gate"), ("U", "up"), ("D", "down"))})

    def run(plan):
        for item in zip(plan[::2], plan[1::2]):
            for u in groups[item[0]]:
                advance(u, int(item[1]))

    small_at = [dict(me)]
    small_cps = []

    def small_step(axis):
        for cp in small_cps:
            cp.wait_recv()
        if small_cps:
            small_at[0] = dict(small_at[0], **{"z" if axis == "x" else "x": ALL})
        at = small_at[0]
        piece = small_full.at[at["z"], at["x"], at["c"]]
        steps = (1,) if axis == "c" else (1, 2, 3)
        small_cps[:] = [links.send(lambda: (piece, piece), axis, s) for s in steps]

    small_step("z")
    run("A0G0U0D0A1G1U1D1")
    small_step("x")
    run("A2G2U2D2A3G3U3D3")
    small_step("c")
    run("A4G4A5U4D4")

    for cp in small_cps:
        cp.wait_recv()
    for k in range(8):
        z, x = k // 2, 2 * (k % 2)
        small_low[:, 128 * k : 128 * k + 128] = (
            small_full[z, x, 0] + small_full[z, x, 1] + small_full[z, x + 1, 0] + small_full[z, x + 1, 1]
        )
    tokens = block_in[...].astype(jnp.float32)
    low = (tokens * norm_scale(tokens) * small_low[3:4]).astype(jnp.bfloat16)
    normed[...] = low
    nft[...] = low.T
    copy(nft, nft_out)
    run("A6")
    for u in groups["A"]:
        for cp in swaps[u]:
            cp.wait_recv()

    def conv_work():
        for q in range(4):
            cols = slice(256 * q, 256 * q + 256)
            cuts = []
            for t in range(3):
                weight = in_full[t, q].reshape(1024, 256)
                cuts.append(dot_nn(normed[...], weight))
            gate_c[:, cols] = cuts[1]
            for t in range(3):
                gates[t, :, cols] = cuts[t].astype(jnp.bfloat16)
            mixed = (cuts[0] * cuts[2]).astype(jnp.bfloat16)
            for m in range(MICRO):
                halo_out[m, :, cols] = mixed[128 * m + 112 : 128 * m + 128]
                ext[m, 8:136, cols] = mixed[128 * m : 128 * m + 128].astype(jnp.float32)
            yield
        sent = links.send_to(lambda: (halo_out, halo_in), lambda: along(me, 1))
        copy(in_full, outputs["in"])
        copy(out_full, outputs["out"])
        yield
        sent.wait_recv()
        keep = (me["z"] * 8 + me["x"] * 2 + me["c"] != 0).astype(jnp.float32)
        for m in range(MICRO):
            ext[m, 0:8] = halo_in[m].astype(jnp.float32)[8:16] * keep
        for m in range(MICRO):
            rows = slice(128 * m, 128 * m + 128)
            conv = small_low[0:1] * ext[m, 8:136]
            for k in range(1, KW):
                conv += small_low[k : k + 1] * ext[m, 8 - k : 136 - k]
            for k in range(KW):
                taps[k, rows] = ext[m, 8 - k : 136 - k].astype(jnp.bfloat16)
            gates[3, rows] = conv.astype(jnp.bfloat16)
            normed[rows] = (gate_c[rows] * conv).astype(jnp.bfloat16)
            yield
        copy(gates, gates_out)
        copy(taps, taps_out)
        got[...] = normed[...].T
        copy(got, got_out)
        yield
        for q in range(4):
            cols = slice(256 * q, 256 * q + 256)
            weight = out_full[q].reshape(1024, 256)
            middle[:, cols] = block_in[:, cols].astype(jnp.float32) + dot_nn(normed[...], weight)
        copy(middle, middle_out)
        yield
        field = middle[...]
        ns[...] = (field * norm_scale(field) * small_low[4:5]).astype(jnp.bfloat16)
        copy(ns, ns_out)
        nst[...] = ns[...].T
        copy(nst, nst_out)
        yield

    work = conv_work()
    for step in (5, 6):
        for key in "GUD":
            for u in groups[key]:
                next(work, None)
                advance(u, step)
    for _ in work:
        pass
    for key in "GUD":
        for u in groups[key]:
            for cp in swaps[u]:
                cp.wait_recv()
    for cp in copies[placed:]:
        cp.wait()
    links.finish()


def forward(weights, small, block_in):
    small_rows = jnp.pad(small.astype(jnp.bfloat16).astype(jnp.float32), ((0, 3), (0, 0)))
    lane = lax.broadcasted_iota(jnp.int32, (8, 128), 1) // 32
    small_own = jnp.where(lane == lax.axis_index("fsdp") % 4, jnp.tile(small_rows, (1, 4)), 0.0)
    in_vmem = pl.BlockSpec(memory_space=pltpu.VMEM)
    anywhere = pl.BlockSpec(memory_space=pl.ANY)
    bf16, f32 = jnp.bfloat16, jnp.float32
    kept = [
        ((256, 1024), bf16),
        ((1024, 256), bf16),
        ((256, 1024), f32),
        ((4, 256, 1024), bf16),
        ((3, 256, 1024), bf16),
        ((1024, 256), bf16),
        ((1024, 256), bf16),
    ]
    outs = pl.pallas_call(
        forward_kernel,
        out_shape=[jax.ShapeDtypeStruct(FULL[name], bf16) for name in MATS]
        + [jax.ShapeDtypeStruct((8, 1024), f32)]
        + [jax.ShapeDtypeStruct(*k) for k in kept],
        in_specs=[in_vmem] * 7,
        out_specs=[anywhere] * 5 + [in_vmem] + [anywhere] * 7,
        scratch_shapes=[pltpu.VMEM(OWN[name], bf16) for name in MATS]
        + [pltpu.VMEM(FULL["in"], bf16), pltpu.VMEM(FULL["out"], bf16)]
        + [pltpu.VMEM((4, 4, 2, 8, 128), f32)]
        + [pltpu.VMEM(*k) for k in kept]
        + [
            pltpu.VMEM((256, 1024), bf16),
            pltpu.VMEM((256, 1024), f32),
            pltpu.VMEM((2, 136, 1024), f32),
            pltpu.VMEM((2, 16, 1024), bf16),
            pltpu.VMEM((2, 16, 1024), bf16),
            pltpu.SemaphoreType.DMA((32,)),
            pltpu.SemaphoreType.DMA((256,)),
            pltpu.SemaphoreType.DMA((256,)),
        ],
        compiler_params=pltpu.CompilerParams(
            collective_id=1, has_side_effects=True, vmem_limit_bytes=VMEM_BYTES
        ),
        name="forward",
    )(*weights, small_own, block_in)
    return outs[0:5], outs[5:]


def norm_back(grad_normed, field, gain):
    scale = norm_scale(field)
    normed = field * scale
    weighted = grad_normed * gain
    grad_field = scale * (weighted - normed * jnp.mean(weighted * normed, axis=-1, keepdims=True))
    return (grad_field, jnp.sum(grad_normed * normed, axis=0, keepdims=True))


def order_of(name, t):
    if name == "gate":
        return SUM_ORDER[(2 * t) % 3]
    if name == "up":
        return SUM_ORDER[(2 * t + 1) % 3]
    return SUM_ORDER[t]


BATCHES = [[("gate", j), ("up", j)] for j in range(FF_BLOCKS)]
BATCHES += [[("down", t) for t in range(3)], [("out", 0), ("out", 1)], [("in", t) for t in range(3)]]
UNITS = [u for batch in BATCHES for u in batch]


def tiles(name):
    return BLOCK[name][0] // 16, BLOCK[name][1] // 128


def tile_count(name):
    return tiles(name)[0] * tiles(name)[1]


def landing(unit):
    k = tile_count(unit[0])
    return [
        ((2, 2, 4, k, 16, 128), (2, 4, 4, k, 16, 128)),
        (None, (3, 4, k, 16, 128)),
        (None, (3, k, 16, 128)),
    ]


def part(ref, unit, at, half=None):
    name, t = unit
    index = [at[a] for a in order_of(*unit)] + [ALL]
    if half is not None:
        size = (4, 4, 4, tile_count(name))
        i = next(i for i in range(4) if index[i] is ALL)
        index[i] = pl.ds(half * (size[i] // 2), size[i] // 2)
    return ref.at[(t,) + tuple(index)]


def run_of(ref, unit, first):
    return ref.at[pl.ds(first, 64 * tile_count(unit[0]))]


LAG = 1
EVERY = {"y": ALL, "z": ALL, "x": ALL}


class Sums:
    def __init__(self, me, links, mine, theirs, outs, staging, slots, slot_sem, land):
        self.me, self.links = me, links
        self.mine, self.theirs, self.outs = mine, theirs, outs
        self.staging, self.slots, self.slot_sem, self.land = staging, slots, slot_sem, land
        self.at = {u: dict(EVERY) for u in UNITS}
        self.swaps, self.loads, self.pending, self.last = {}, {}, {}, []
        self.users = []

    def first(self, unit, slots):
        k = UNITS.index(unit)
        return 128 * (k % slots) if k < 2 * FF_BLOCKS else 384 * (k % (slots // 2))

    def room(self, unit):
        first, count = self.first(unit, 4), 64 * tile_count(unit[0])
        for low, high, user in self.users:
            if low < first + count and first < high and id(user) not in self.links.done:
                self.links.left(user)
        return first

    def swap(self, unit):
        first, count = self.first(unit, 4), 64 * tile_count(unit[0])

        def ends():
            place = run_of(self.theirs[unit[0]], unit, count * unit[1])
            return run_of(self.staging, unit, first), place

        self.swaps[unit] = self.links.send(ends, "c", 1)
        self.users.append((first, first + count, self.swaps[unit]))

    def load(self, unit):
        self.swaps[unit].wait_recv()
        src = run_of(self.theirs[unit[0]], unit, 64 * tile_count(unit[0]) * unit[1])
        dst = run_of(self.slots, unit, self.first(unit, 2))
        cp = pltpu.make_async_copy(src, dst, self.slot_sem.at[UNITS.index(unit)])
        cp.start()
        self.loads[unit] = cp

    def join(self, unit):
        self.loads[unit].wait()
        total = part(self.mine[unit[0]], unit, EVERY)
        first, k = self.first(unit, 2), tile_count(unit[0])

        def step(i, carry):
            spot = (i // 4, i % 4)
            fresh = self.slots[pl.ds(first + 4 * k * i, 4 * k)].reshape(4, k, 16, 128)
            total[spot] = total[spot] + fresh
            return carry

        lax.fori_loop(0, 16, step, 0, unroll=2)
        self.start(unit, 0)

    def add(self, unit, p, at, half, *landed):
        ref = part(self.mine[unit[0]], unit, at, half)
        if p > 0:
            self.add_block(ref, ALL, *landed)
            return

        def step(i, carry):
            self.add_block(ref, i, *landed)
            return carry

        lax.fori_loop(0, 4 if half is None else 2, step, 0, unroll=2)

    def add_block(self, ref, i, *landed):
        if len(landed) == 1:
            ref[i] = ref[i] + landed[0][i]
            return
        total = ref[i].astype(jnp.float32)
        for value in landed:
            total = total + value[i].astype(jnp.float32)
        ref[i] = total.astype(jnp.bfloat16)

    def spot(self, at, axis, by):
        return dict(at, **{axis: (self.me[axis] + by) % 4})

    def start(self, unit, p):
        axis = order_of(*unit)[p]
        at = self.at[unit]
        halves, blocks = self.land[unit][p]
        ref = self.mine[unit[0]]
        if p > 0:

            def block_ends(by):
                return lambda: (part(ref, unit, self.spot(at, axis, by)), blocks.at[by - 1])

            self.pending[unit] = [self.links.send(block_ends(by), axis, by) for by in (1, 2, 3)]
            return

        def ends(side):
            return lambda: (part(ref, unit, self.spot(at, axis, 2), side), halves.at[side])

        self.pending[unit] = [
            self.links.send(ends(0), axis, 1),
            self.links.send(ends(1), axis, 3),
        ]

    def middle(self, unit, p):
        axis = order_of(*unit)[p]
        at = self.at[unit]
        halves, blocks = self.land[unit][p]
        ref = self.mine[unit[0]]
        sends = []

        def ends(side, by):
            return lambda: (part(ref, unit, self.spot(at, axis, by)), blocks.at[side])

        for side, by in enumerate((1, 3)):
            self.pending[unit][side].wait_recv()
            self.add(unit, p, self.spot(at, axis, by), side, halves.at[side])
            sends.append(self.links.send(ends(side, by), axis, by))
        self.pending[unit] = sends

    def end(self, unit, p):
        axis = order_of(*unit)[p]
        blocks = self.land[unit][p][1]
        for cp in self.pending[unit]:
            cp.wait_recv()
        self.at[unit] = dict(self.at[unit], **{axis: self.me[axis]})
        self.add(unit, p, self.at[unit], None, *[blocks.at[i] for i in range(blocks.shape[0])])
        if p < 2:
            self.start(unit, p + 1)
            return

        def mine_out():
            return self.outs[unit[0]].at[unit[1], self.me["y"]]

        mine_out()[...] = part(self.mine[unit[0]], unit, self.at[unit])[...]
        for by in (1, 2, 3):
            self.last.append(self.links.send(lambda: (mine_out(), mine_out()), "y", by))

    def stage(self, s, batch):
        for unit in batch:
            if s == 0:
                self.middle(unit, 0)
            else:
                self.end(unit, s - 1)


def backward_kernel(*refs):
    refs = list(refs)
    take = lambda n: [refs.pop(0) for _ in range(n)]
    ns, g, small_low = take(3)
    nst_hbm, wg, wu, wd, w_in, w_out = take(6)
    middle_hbm, tokens_hbm, gates_hbm, taps_hbm, nft_hbm, got_hbm = take(6)
    outs = dict(zip(MATS, take(5)))
    small_out, block_out, input_grad = take(3)
    theirs = dict(zip(MATS, take(5)))
    mine = dict(zip(MATS, take(5)))
    land = {u: [tuple(take(2)), (None, *take(1)), (None, *take(1))] for u in UNITS}
    staging, slots, hidden_t, grad_ns, ff_out, nst = take(6)
    halo_out, halo_in, small_land = take(3)
    local_sem, slot_sem, send_sem, recv_sem = take(4)
    me = coords()
    links = Links(me, send_sem, recv_sem)
    sums = Sums(me, links, mine, theirs, outs, staging, slots, slot_sem, land)

    def first_loads(wg_s, wu_s, wd_s):
        def fetch(j):
            s = j % 2
            pairs = [
                (wg.at[j], wg_s.at[s]),
                (wu.at[j], wu_s.at[s]),
                (wd.at[:, pl.ds(512 * j, 512)], wd_s.at[s]),
            ]
            cps = [
                pltpu.make_async_copy(a, b, local_sem.at[3 * s + i]) for i, (a, b) in enumerate(pairs)
            ]
            for cp in cps:
                cp.start()
            return cps

        return fetch

    def drive(tick, work):
        tasks = []
        if 0 <= tick - 1 < len(BATCHES):
            batch = BATCHES[tick - 1]
            ahead = 2 if tick - 1 < FF_BLOCKS else 1
            for unit in batch[:ahead]:
                sums.load(unit)

            def joins():
                for i, unit in enumerate(batch):
                    if i >= ahead:
                        sums.load(unit)
                    sums.join(unit)

            tasks.append(joins)
        for s in range(4):
            if 0 <= tick - 1 - LAG * (s + 1) < len(BATCHES):
                tasks.append(functools.partial(sums.stage, s, BATCHES[tick - 1 - LAG * (s + 1)]))
        for _ in work if work is not None else ():
            for _ in range(2):
                if tasks:
                    tasks.pop(0)()
        for task in tasks:
            task()

    def spread(name, t, value, half):
        unit = (name, t)
        rows, cols = BLOCK[name]
        down, across = tiles(name)
        first = sums.room(unit) if half == 1 else None
        for q in range(4):
            for h in range(across):
                for z in range(4):
                    piece = value[4 * rows * z : 4 * rows * (z + 1), cols * q + 128 * h :][:, 0:128]
                    piece = piece.astype(jnp.bfloat16).reshape(4, down, 16, 128)
                    kinds = slice(down * h, down * h + down)
                    if half == 0:
                        at = {"z": z, "y": q, "x": ALL}
                        spot = tuple(at[a] for a in order_of(*unit))
                        mine[name][(t,) + spot + (kinds,)] = piece
                        continue
                    for x in range(4):
                        at = {"z": z, "y": q, "x": x}
                        i, j, k = (at[a] for a in order_of(*unit))
                        start = first + (16 * i + 4 * j + k) * down * across + down * h
                        staging[start : start + down] = piece[x]
        if half == 1:
            sums.swap((name, t))

    def ff_block(j, wg_s, wu_s, wd_s, fetch, fetched):
        for cp in fetched[j]:
            cp.wait()
        if j + 1 < FF_BLOCKS:
            fetched[j + 1] = fetch(j + 1)
        s = j % 2
        gate_w = jnp.concatenate([wg_s[s, q] for q in range(4)], axis=1)
        up_w = jnp.concatenate([wu_s[s, q] for q in range(4)], axis=1)
        gate_pre = dot_nn(ns[...], gate_w)
        up_pre = dot_nn(ns[...], up_w)
        grad_hidden = dot_nt(g[:, 0:256], wd_s[s, 0])
        for q in range(1, 4):
            grad_hidden += dot_nt(g[:, 256 * q : 256 * q + 256], wd_s[s, q])
        sig = jax.nn.sigmoid(gate_pre)
        silu = gate_pre * sig
        hidden = (silu * up_pre).astype(jnp.bfloat16)
        grad_gate = (grad_hidden * up_pre * sig * (1.0 + gate_pre * (1.0 - sig))).astype(
            jnp.bfloat16
        )
        grad_up = (grad_hidden * silu).astype(jnp.bfloat16)
        for half in (1, 0):
            spread("gate", j, dot_nn(nst[half].reshape(512, 256), grad_gate), half)
            spread("up", j, dot_nn(nst[half].reshape(512, 256), grad_up), half)
        yield
        turned = hidden.T
        for k in range(32):
            row = 512 * j + 16 * k
            f, r = row // 144, row % 144
            hidden_t[f // 2, f % 2, r : r + 16, :] = turned[16 * k : 16 * k + 16]
        fresh = dot_nt(grad_gate, gate_w) + dot_nt(grad_up, up_w)
        if j == 0:
            grad_ns[...] = fresh
        else:
            grad_ns[...] += fresh
        for q in range(4):
            cols = slice(256 * q, 256 * q + 256)
            if j == 0:
                ff_out[:, cols] = dot_nn(hidden, wd_s[s, q])
            else:
                ff_out[:, cols] += dot_nn(hidden, wd_s[s, q])
        yield

    def feed_forward(wg_s, wu_s, wd_s):
        fetch = first_loads(wg_s, wu_s, wd_s)
        by_core = [
            pltpu.make_async_copy(nst_hbm.at[:, (me["c"] + h) % 2], nst.at[h], local_sem.at[6 + h])
            for h in (0, 1)
        ]
        for cp in by_core:
            cp.start()
        fetched = {0: fetch(0)}
        meet(me)
        for cp in by_core:
            cp.wait()
        for j in range(FF_BLOCKS):
            drive(j, ff_block(j, wg_s, wu_s, wd_s, fetch, fetched))

    pl.run_scoped(
        feed_forward,
        pltpu.VMEM((2, 4, 1024, 128), jnp.bfloat16),
        pltpu.VMEM((2, 4, 1024, 128), jnp.bfloat16),
        pltpu.VMEM((2, 4, 512, 256), jnp.bfloat16),
    )

    def give_input_grad():
        return pltpu.make_async_copy(ff_out, input_grad, local_sem.at[15])

    small_at = [0]
    small_cps = []

    def small_send(axis):
        steps = (1,) if axis == "c" else (1, 2, 3)
        first = small_at[0]
        small_at[0] += len(steps)
        small_cps[:] = [
            links.send(lambda s=s: (small_out, small_land.at[first + s - 1]), axis, s)
            for s in steps
        ]

    def small_take():
        first = small_at[0] - len(small_cps)
        for cp in small_cps:
            cp.wait_recv()
        for cp in small_cps:
            links.left(cp)
        total = small_out[...]
        for s in range(len(small_cps)):
            total = total + small_land[first + s]
        small_out[...] = total

    def conv_branch(middle, tokens, gates, taps_in, nft, got, wi_s, conv_ext, grad_proj):
        wo_s, grad_in = wi_s.at[1], ff_out
        sources = [middle_hbm, tokens_hbm, gates_hbm, taps_hbm, w_out]
        places = [middle, tokens, gates, taps_in, wo_s]
        for h in (0, 1):
            sources += [nft_hbm.at[:, (me["c"] + h) % 2], got_hbm.at[:, (me["c"] + h) % 2]]
            places += [nft.at[h], got.at[h]]
        cps = [pltpu.make_async_copy(a, b, local_sem.at[i]) for i, (a, b) in enumerate(zip(sources, places))]
        for cp in cps:
            cp.start()
        fetched = {}

        def fetch(t):
            fetched[t] = pltpu.make_async_copy(
                w_in.at[pl.ds(4 * t, 4)], wi_s.at[t % 2], local_sem.at[10 + t]
            )
            fetched[t].start()

        fetch(0)

        def down_work():
            for t in range(3):
                for half in (1, 0):
                    c = (me["c"] + half) % 2
                    left = hidden_t[:, c, 48 * t : 48 * t + 48, :].reshape(768, 256)
                    spread("down", t, dot_nn(left, g[...]), half)
                yield

        drive(9, down_work())
        for cp in cps:
            cp.wait()

        def out_work():
            gain_second = small_low[4:5]
            block_out[...] = (middle[...] + ff_out[...]).astype(jnp.bfloat16)
            grad_norm, grad_gain = norm_back(grad_ns[...], middle[...], gain_second)
            small_out[4:5] = grad_gain
            grad_middle = g[...].astype(jnp.float32) + grad_norm
            middle[...] = grad_middle
            grad_branch = grad_middle.astype(jnp.bfloat16)
            for half in (1, 0):
                whole = dot_nn(got[half].reshape(512, 256), grad_branch).reshape(16, 2, 16, 1024)
                for t in range(2):
                    spread("out", t, whole[:, t].reshape(256, 1024), half)
            yield
            grad_gated = dot_nt(grad_branch[:, 0:256], wo_s[0])
            for q in range(1, 4):
                grad_gated += dot_nt(grad_branch[:, 256 * q : 256 * q + 256], wo_s[q])
            grad_conv = (grad_gated * gates[1].astype(jnp.float32)).astype(jnp.bfloat16)
            for m in range(MICRO):
                halo_out[m] = grad_conv[128 * m : 128 * m + 16]
            sent = links.send_to(lambda: (halo_out, halo_in), lambda: along(me, 31))
            grad_proj[:, 1024:2048] = (grad_gated * gates[3].astype(jnp.float32)).astype(jnp.bfloat16)
            wide = grad_conv.astype(jnp.float32)
            for m in range(MICRO):
                conv_ext[m, 0:128] = wide[128 * m : 128 * m + 128]
            for k in range(KW):
                small_out[k : k + 1] = jnp.sum(
                    wide * taps_in[k].astype(jnp.float32), axis=0, keepdims=True
                )
            yield
            sent.wait_recv()
            keep = (me["z"] * 8 + me["x"] * 2 + me["c"] != 31).astype(jnp.float32)
            for m in range(MICRO):
                conv_ext[m, 128:136] = halo_in[m].astype(jnp.float32)[0:8] * keep
            for m in range(MICRO):
                mixed = small_low[0:1] * conv_ext[m, 0:128]
                for k in range(1, KW):
                    mixed += small_low[k : k + 1] * conv_ext[m, k : k + 128]
                rows = slice(128 * m, 128 * m + 128)
                grad_proj[rows, 0:1024] = (mixed * gates[2, rows].astype(jnp.float32)).astype(
                    jnp.bfloat16
                )
                grad_proj[rows, 2048:3072] = (mixed * gates[0, rows].astype(jnp.float32)).astype(
                    jnp.bfloat16
                )

        drive(10, out_work())
        fetch(1)

        def in_work():
            for t in range(3):
                cols = slice(1024 * t, 1024 * t + 1024)
                for half in (1, 0):
                    spread("in", t, dot_nn(nft[half].reshape(512, 256), grad_proj[:, cols]), half)
                yield

        drive(11, in_work())

        def token_work():
            for t in range(3):
                fetched[t].wait()
                for q in range(4):
                    cols = slice(256 * (4 * t + q), 256 * (4 * t + q) + 256)
                    fresh = dot_nt(grad_proj[:, cols], wi_s[t % 2, q])
                    if t == 0 and q == 0:
                        grad_in[...] = fresh
                    else:
                        grad_in[...] += fresh
                if t == 0:
                    fetch(2)
                yield
            x = tokens[...].astype(jnp.float32)
            grad_norm, grad_gain = norm_back(grad_in[...], x, small_low[3:4])
            small_out[3:4] = grad_gain
            small_out[5:8] = jnp.zeros((3, 1024), jnp.float32)
            grad_in[...] = middle[...] + grad_norm
            give_input_grad().start()
            small_send("c")

        drive(12, token_work())

    pl.run_scoped(
        conv_branch,
        pltpu.VMEM((256, 1024), jnp.float32),
        pltpu.VMEM((256, 1024), jnp.bfloat16),
        pltpu.VMEM((4, 256, 1024), jnp.bfloat16),
        pltpu.VMEM((3, 256, 1024), jnp.bfloat16),
        pltpu.VMEM((2, 16, 32, 256), jnp.bfloat16),
        pltpu.VMEM((2, 16, 32, 256), jnp.bfloat16),
        pltpu.VMEM((2, 4, 1024, 256), jnp.bfloat16),
        pltpu.VMEM((2, 136, 1024), jnp.float32),
        pltpu.VMEM((256, 3072), jnp.bfloat16),
    )
    for i, axis in enumerate("xzy"):
        drive(13 + i, None)
        small_take()
        small_send(axis)
    drive(16, None)
    small_take()
    for tick in range(17, len(BATCHES) + 1 + 4 * LAG):
        drive(tick, None)
    for cp in sums.last:
        cp.wait_recv()
    give_input_grad().wait()
    links.finish()


def backward(ns, g, small_low, nst, w_gate, w_up, w_down, w_in, w_out, middle, tokens, *rest):
    in_vmem = pl.BlockSpec(memory_space=pltpu.VMEM)
    anywhere = pl.BlockSpec(memory_space=pl.ANY)
    tiled = {}
    for name in MATS:
        pieces = FULL[name][0 if name in BY_THIRD else 4]
        tiled[name] = (pieces, tile_count(name))
    scratch = [pltpu.VMEM((n, 4, 4, 4, k, 16, 128), jnp.bfloat16) for n, k in tiled.values()]
    for u in UNITS:
        for halves, blocks in landing(u):
            shapes = [blocks] if halves is None else [halves, blocks]
            scratch += [pltpu.VMEM(shape, jnp.bfloat16) for shape in shapes]
    scratch += [
        pltpu.VMEM((768, 16, 128), jnp.bfloat16),
        pltpu.VMEM((384, 16, 128), jnp.bfloat16),
        pltpu.VMEM((16, 2, 144, 256), jnp.bfloat16),
        pltpu.VMEM((256, 1024), jnp.float32),
        pltpu.VMEM((256, 1024), jnp.float32),
        pltpu.VMEM((2, 16, 32, 256), jnp.bfloat16),
        pltpu.VMEM((2, 16, 1024), jnp.bfloat16),
        pltpu.VMEM((2, 16, 1024), jnp.bfloat16),
        pltpu.VMEM((10, 8, 1024), jnp.float32),
        pltpu.SemaphoreType.DMA((16,)),
        pltpu.SemaphoreType.DMA((len(UNITS),)),
        pltpu.SemaphoreType.DMA((480,)),
        pltpu.SemaphoreType.DMA((480,)),
    ]
    outs = pl.pallas_call(
        backward_kernel,
        out_shape=[jax.ShapeDtypeStruct((n, 4, k, 16, 128), jnp.bfloat16) for n, k in tiled.values()]
        + [
            jax.ShapeDtypeStruct((8, 1024), jnp.float32),
            jax.ShapeDtypeStruct((256, 1024), jnp.bfloat16),
            jax.ShapeDtypeStruct((256, 1024), jnp.float32),
        ]
        + [jax.ShapeDtypeStruct((n * 64 * k, 16, 128), jnp.bfloat16) for n, k in tiled.values()],
        in_specs=[in_vmem] * 3 + [anywhere] * 12,
        out_specs=[in_vmem] * 7 + [anywhere] * 6,
        scratch_shapes=scratch,
        compiler_params=pltpu.CompilerParams(
            collective_id=2, has_side_effects=True, vmem_limit_bytes=VMEM_BYTES
        ),
        name="backward",
    )(ns, g, small_low, nst, w_gate, w_up, w_down, w_in, w_out, middle, tokens, *rest)
    return outs[0:5], outs[5], outs[6], outs[7]


def adam_update(weight, first, second, gradient, step_rate, decay_rate):
    first_new = beta_one * first + (1.0 - beta_one) * gradient
    second_new = beta_two * second + (1.0 - beta_two) * gradient * gradient
    corrected = (
        first_new
        / (1.0 - beta_one**STEP)
        / (jnp.sqrt(second_new / (1.0 - beta_two**STEP)) + adam_eps)
    )
    return (weight - step_rate * (corrected + decay_rate * weight), first_new, second_new)


def adam_kernel(*refs):
    sources = [dict(zip(MATS, refs[5 * i : 5 * i + 5])) for i in range(4)]
    results = [dict(zip(MATS, refs[20 + 5 * i : 25 + 5 * i])) for i in range(3)]
    weights, firsts, seconds, sums = sources

    def update(name):
        rows, cols = BLOCK[name]
        down, across = tiles(name)
        for t in range(sums[name].shape[0]):
            for q in range(4):
                for h in range(across):
                    if name in BY_THIRD:
                        top, left = 0, (4 * t + q) * cols + 128 * h
                    else:
                        top, left = t * rows, q * cols + 128 * h
                    spot = (slice(top, top + rows), slice(left, left + 128))
                    gradient = sums[name][t, q, down * h : down * h + down].reshape(rows, 128)
                    new = adam_update(
                        weights[name][spot],
                        firsts[name][spot],
                        seconds[name][spot],
                        gradient.astype(jnp.float32),
                        rate_matrix,
                        weight_decay,
                    )
                    for result, value in zip(results, new):
                        result[name][spot] = value

    for name in ("in", "gate", "up", "down"):
        update(name)

    @pl.when(pl.program_id(0) == 0)
    def _():
        update("out")


def adam(weights, firsts, seconds, sums):
    shard = {
        "in": pl.BlockSpec((32, 1024), lambda i: (0, i)),
        "out": pl.BlockSpec((32, 1024), lambda i: (0, 0)),
        "gate": pl.BlockSpec((32, 1536), lambda i: (0, i)),
        "up": pl.BlockSpec((32, 1536), lambda i: (0, i)),
        "down": pl.BlockSpec((48, 1024), lambda i: (i, 0)),
    }
    pieces = {
        "in": pl.BlockSpec((1, 4, 4, 16, 128), lambda i: (i, 0, 0, 0, 0)),
        "out": pl.BlockSpec((2, 4, 2, 16, 128), lambda i: (0, 0, 0, 0, 0)),
        "gate": pl.BlockSpec((3, 4, 2, 16, 128), lambda i: (i, 0, 0, 0, 0)),
        "up": pl.BlockSpec((3, 4, 2, 16, 128), lambda i: (i, 0, 0, 0, 0)),
        "down": pl.BlockSpec((1, 4, 6, 16, 128), lambda i: (i, 0, 0, 0, 0)),
    }
    in_order = [shard[name] for name in MATS]
    outs = pl.pallas_call(
        adam_kernel,
        grid=(3,),
        in_specs=in_order * 3 + [pieces[name] for name in MATS],
        out_specs=in_order * 3,
        out_shape=[jax.ShapeDtypeStruct(w.shape, jnp.float32) for w in weights] * 3,
        compiler_params=pltpu.CompilerParams(vmem_limit_bytes=VMEM_BYTES),
        name="adam",
    )(*weights, *firsts, *seconds, *sums)
    return outs[0:5], outs[5:10], outs[10:15]


def body(
    block_input,
    cotangent,
    in_weight,
    out_weight,
    gate_weight,
    up_weight,
    down_weight,
    small_params,
    in_first,
    out_first,
    gate_first,
    up_first,
    down_first,
    small_first,
    in_second,
    out_second,
    gate_second,
    up_second,
    down_second,
    small_second,
):
    rows = block_input.shape[1]
    tokens = block_input.reshape(256, 1024)
    full, kept = forward(
        (in_weight, out_weight, gate_weight, up_weight, down_weight), small_params, tokens
    )
    small_low, ns, nst, middle, gates, taps, nft, got = kept
    cuts = (16, 2, 32, 256)
    summed, small_sum, block_out, input_grad = backward(
        ns,
        cotangent.reshape(256, 1024),
        small_low,
        nst.reshape(cuts),
        full[2].reshape(9, 4, 1024, 128),
        full[3].reshape(9, 4, 1024, 128),
        full[4].reshape(4, 4608, 256),
        full[0].reshape(12, 1024, 256),
        full[1].reshape(4, 1024, 256),
        middle,
        tokens,
        gates,
        taps,
        nft.reshape(cuts),
        got.reshape(cuts),
    )
    position = lax.axis_index("fsdp")
    small_mine = lax.dynamic_slice(small_sum, (0, position * 32), (5, 32))
    new_weights, new_firsts, new_seconds = adam(
        (in_weight, out_weight, gate_weight, up_weight, down_weight),
        (in_first, out_first, gate_first, up_first, down_first),
        (in_second, out_second, gate_second, up_second, down_second),
        summed,
    )
    new_small = adam_update(small_params, small_first, small_second, small_mine, rate_small, 0.0)
    return (
        block_out.reshape(MICRO, rows, 1024),
        input_grad.reshape(MICRO, rows, 1024),
        *new_weights,
        new_small[0],
        *new_firsts,
        new_small[1],
        *new_seconds,
        new_small[2],
    )


def solution(mesh):
    acts = P(None, ("dp", "fsdp"), None)
    params = (P("fsdp", None),) * 5 + (P(None, "fsdp"),)
    return jax.shard_map(
        body,
        mesh=mesh,
        in_specs=(acts, acts) + params * 3,
        out_specs=(acts, acts) + params * 3,
        check_vma=False,
    )
```
